32 devices in a mesh: blk: 8 (over y, x, core), head: 4 (over z).
Axes of the slice: x: 2, y: 2, z: 4, core: 2. Of those that a mesh axis runs over, the one named last changes fastest.
Arguments:
- tokens: bfloat16 [8, 1024, 768], P(None, ('blk', 'head')), may hold values from -6 to 6
- chain_id: int32 [1024], P(('blk', 'head')), may hold values from 0 to 3, never falling along the last dimension, each value on 1 to 512 neighbouring positions
- hotspots: int32 [16], replicated, may hold values from 0 to 1023
- chain_embed: bfloat16 [4, 768], replicated, may hold values from -6 to 6
- hot_embed: bfloat16 [768], replicated, may hold values from -6 to 6
- w_proj: bfloat16 [768, 3072], P(None, 'head'), may hold values from -0.21875 to 0.21875
- pair_bias: bfloat16 [16, 1024, 1024], P('head', 'blk'), may hold values from -400 to 400
- w_out: bfloat16 [768, 768], P('head'), may hold values from -0.21875 to 0.21875
Outputs:
- update: bfloat16 [8, 1024, 768], P(None, ('blk', 'head'))
The draws below stay inside these ranges and needn't reach their ends.
Inputs may be any that keep to these rules, and one draw needn't show every extreme that they name: `chain_id`: chain ids never fall along the tokens; one chain has exactly 512 tokens. `hotspots`: positions may repeat.
All inputs are finite; a program needn't handle non-finite values.
Results may differ from the reference program's by a relative error of at most 0.02.
Values may be sent and summed in bfloat16 or wider, within the bound.
A program may use at most 64 MiB of HBM per device.

```python
import math
import jax
import jax.numpy as jnp
import numpy as np
from jax import lax

D = 768
H = 16
HD = 48
SAMPLES = 8
CHAINS = 4
HOT = 16
N = 1024


def draw_pair_bias(key, part):
    key = jax.random.fold_in(key, 11)
    row_key, col_key, base_key = jax.random.split(key, 3)
    row_scale = jnp.exp(jax.random.uniform(row_key, (H, N, 1), jnp.float32, jnp.log(0.5), jnp.log(1.5)))
    col_scale = jnp.exp(jax.random.uniform(col_key, (H, 1, N), jnp.float32, jnp.log(0.3), jnp.log(3.0)))

    def one_head(inputs):
        head_index, row_part, col_part = inputs
        head_key = jax.random.fold_in(base_key, head_index)
        return jax.random.normal(head_key, (N, N), jnp.float32) * row_part * col_part
    full = lax.map(one_head, (jnp.arange(H, dtype=jnp.int32), row_scale, col_scale))
    return full.astype(jnp.bfloat16)


def touch_ends(values, key, least, top_value):
    dims = values.shape
    place = [jax.random.randint(jax.random.fold_in(key, axis), (), 0, dims[axis]) for axis in range(len(dims))]
    values = values.at[tuple(place)].set(least)
    longest = dims.index(max(dims))
    place[longest] = (place[longest] + 1) % dims[longest]
    return values.at[tuple(place)].set(top_value)


def shard_levels(key, shape, cuts, least, largest):
    def one(axis_at, shards_of):
        heights = jax.random.uniform(jax.random.fold_in(jax.random.fold_in(key, 6), axis_at), (shards_of,), jnp.float32, least / len(cuts), largest / len(cuts))
        return jnp.repeat(jnp.exp(heights), shape[axis_at] // shards_of).reshape((-1,) + (1,) * (len(shape) - axis_at - 1))

    level = one(*cuts[0])
    for cut in cuts[1:]:
        level = level * one(*cut)
    return level


def profile(amount, total, limit, slope):
    loads = [(1 << 20) // math.isqrt(grade ** slope) + 1 for grade in range(2, amount + 1)]
    surplus, given = total - limit - (amount - 1), [1] * (amount - 1)
    while surplus > 0:
        free = [i for i in range(amount - 1) if given[i] < limit]
        pool, remaining = sum([loads[i] for i in free]), surplus
        for i in free:
            more = min(limit - given[i], max(1, remaining * loads[i] // pool), surplus)
            given[i] = given[i] + more
            surplus = surplus - more
    return np.array([limit] + given)


def ragged_sizes(own_key, amount, total, reach, lean):
    if amount == 2:
        one = jax.random.randint(own_key, (), max(1, total - reach), min(reach, total - 1) + 1)
        return jnp.stack([one, total - one])
    tallies = jnp.asarray(profile(amount, total, reach, lean), jnp.int32)
    couples = (amount - 1) // 2
    source_of, receiver = tallies[1:1 + 2 * couples:2], tallies[2:2 + 2 * couples:2]
    room = jnp.minimum(source_of - 1, reach - receiver)
    moved = jax.random.randint(jax.random.fold_in(own_key, 1), (couples,), 0, 1 << 20) % (room + 1)
    tallies = tallies.at[1:1 + 2 * couples:2].set(source_of - moved).at[2:2 + 2 * couples:2].set(receiver + moved)
    return tallies[jax.random.permutation(jax.random.fold_in(own_key, 2), amount)]


def noise(stream_key, dims, width, reach, cuts=(), kind=jnp.bfloat16):
    values = jax.random.normal(stream_key, dims, jnp.float32) * width
    if len(cuts) > 0:
        values = shard_levels(stream_key, dims, cuts, -0.22, 0.18) * values
    return jnp.clip(values, min=-reach, max=reach).astype(kind)


def setup_inputs(seed: int = 0) -> dict:
    arg_keys = jax.random.split(jax.random.key(seed), 9)
    tokens = noise(arg_keys[0], (SAMPLES, N, D), 1.0, 6.0, ((1, 32),))
    chain_id = jnp.searchsorted(jnp.cumsum(ragged_sizes(arg_keys[1], CHAINS, N, N // 2, 0)), jnp.arange(N), side="right").astype(jnp.int32)
    hotspots = touch_ends(jax.random.randint(arg_keys[2], (HOT,), 0, N), jax.random.fold_in(arg_keys[2], 1), 0, N - 1).astype(jnp.int32)
    chain_embed = noise(arg_keys[3], (CHAINS, D), 1.0, 6.0)
    hot_embed = noise(arg_keys[4], (D,), 1.0, 6.0)
    w_proj = noise(arg_keys[5], (D, 4 * D), D ** -0.5, 0.21875, ((1, 4),))
    pair_bias = draw_pair_bias(jax.random.fold_in(arg_keys[8], 71), 0)
    w_out = noise(arg_keys[7], (D, D), D ** -0.5, 0.21875, ((0, 4),))
    return {"tokens": tokens, "chain_id": chain_id, "hotspots": hotspots, "chain_embed": chain_embed, "hot_embed": hot_embed, "w_proj": w_proj, "pair_bias": pair_bias, "w_out": w_out}


def attend_head(inputs):
    queries, keys, values, gating, bias_head = inputs
    block_rows = 512 if N % 512 == 0 else N
    blocks = N // block_rows
    query_blocks = jnp.moveaxis(queries.reshape(SAMPLES, blocks, block_rows, HD), 1, 0)
    gate_blocks = jnp.moveaxis(gating.reshape(SAMPLES, blocks, block_rows, HD), 1, 0)
    bias_blocks = bias_head.reshape(blocks, block_rows, N)

    def attend_rows(parts):
        query_rows, bias_rows, gate_rows = parts
        scores = jnp.einsum('sqd,skd->sqk', query_rows.astype(jnp.float32), keys.astype(jnp.float32))
        scores = scores + bias_rows.astype(jnp.float32)[None]
        row_max = lax.optimization_barrier(jnp.max(scores, axis=-1, keepdims=True))
        probs = jnp.exp(scores - row_max)
        row_sum = lax.optimization_barrier(jnp.sum(probs, axis=-1))
        rounded = probs.astype(jnp.bfloat16).astype(jnp.float32)
        weighted = jnp.einsum('sqk,skd->sqd', rounded, values.astype(jnp.float32))
        return (weighted / row_sum[..., None] * gate_rows).astype(jnp.bfloat16)
    result = lax.map(attend_rows, (query_blocks, bias_blocks, gate_blocks))
    return jnp.moveaxis(result, 0, 1).reshape(SAMPLES, N, HD)

def reference(tokens, chain_id, hotspots, chain_embed, hot_embed, w_proj, pair_bias, w_out):
    onehot = (chain_id[:, None] == jnp.arange(CHAINS, dtype=jnp.int32)[None, :]).astype(jnp.float32)
    is_hot = jnp.any(jnp.arange(N, dtype=jnp.int32)[:, None] == hotspots[None, :], axis=1).astype(jnp.float32)
    condition = lax.optimization_barrier(jnp.sum(onehot[:, :, None] * chain_embed.astype(jnp.float32)[None], axis=1))
    condition = condition + is_hot[:, None] * hot_embed.astype(jnp.float32)[None, :]
    shifted = tokens.astype(jnp.float32) + condition[None]
    average = lax.optimization_barrier(jnp.mean(shifted, axis=-1, keepdims=True))
    spread = lax.optimization_barrier(jnp.mean((shifted - average) ** 2, axis=-1, keepdims=True))
    normed = ((shifted - average) * lax.rsqrt(spread + 1e-05)).astype(jnp.bfloat16)
    proj = jnp.dot(normed.reshape(SAMPLES * N, D), w_proj, preferred_element_type=jnp.float32)
    proj = proj.reshape(SAMPLES, N, H, 4, HD)
    queries = (proj[:, :, :, 0] * (1.0 / HD ** 0.5)).astype(jnp.bfloat16)
    keys = proj[:, :, :, 1].astype(jnp.bfloat16)
    values = proj[:, :, :, 2].astype(jnp.bfloat16)
    gating = jax.nn.sigmoid(proj[:, :, :, 3])
    per_head = lax.map(attend_head, (jnp.moveaxis(queries, 2, 0), jnp.moveaxis(keys, 2, 0), jnp.moveaxis(values, 2, 0), jnp.moveaxis(gating, 2, 0), pair_bias))
    gated = jnp.moveaxis(per_head, 0, 2).reshape(SAMPLES * N, D)
    update = jnp.dot(gated, w_out, preferred_element_type=jnp.float32)
    return update.astype(jnp.bfloat16).reshape(SAMPLES, N, D)
```

```python
import functools
import jax
import jax.numpy as jnp
from jax import lax
from jax.experimental import pallas as pl
from jax.experimental.pallas import tpu as pltpu
from jax.sharding import PartitionSpec as P

HD = 48
MESH = pl.DeviceIdType.MESH


def flip(index, bits, count):
    total = 0
    weight = 1
    while weight < count:
        bit = (index // weight) % 2
        total = total + ((1 - bit) if (bits // weight) % 2 else bit) * weight
        weight *= 2
    return total


def low_bit(r):
    return r & -r


def high_bit(r):
    return 1 << (r.bit_length() - 1)


def kernel(
    n, nb, chain_ref, hot_ref, tok_ref, cemb_ref, hemb_ref, w_ref, bias_ref, wout_ref, out_ref,
    x_all, table, cond, w_t, kv, q_all, gate_all, gout, gin, wo,
    xs_sem, xr_sem, ws_sem, wr_sem, ks_sem, kr_sem, gs_sem, gr_sem,
):
    samples, td, width = tok_ref.shape
    hh = bias_ref.shape[0]
    tb = n * td
    cols = hh * HD
    z = lax.axis_index("head")
    b = lax.axis_index("blk")
    bits = [1 << k for k in range(nb.bit_length() - 1)]

    barrier = pltpu.get_barrier_semaphore()
    for o in range(1, n):
        pl.semaphore_signal(
            barrier, inc=1, device_id={"blk": b, "head": (z + o) % n}, device_id_type=MESH
        )
    for bit in bits:
        pl.semaphore_signal(
            barrier, inc=1, device_id={"blk": flip(b, bit, nb), "head": z}, device_id_type=MESH
        )

    def line_copy(at, send, recv, block, to):
        return pltpu.make_async_remote_copy(
            src_ref=at(block), dst_ref=at(block), send_sem=send, recv_sem=recv,
            device_id={"blk": b, "head": to}, device_id_type=MESH,
        )

    def line_send(at, send, recv, d, act):
        @pl.when((z - d + 1 >= 0) & (z + 1 < n))
        def _():
            act(line_copy(at, send(0, d), recv(0, d), z - d + 1, z + 1))

        @pl.when((z + d - 1 < n) & (z >= 1))
        def _():
            act(line_copy(at, send(1, d), recv(1, d), z + d - 1, z - 1))

    def line_recv(at, send, recv, d):
        @pl.when(z - d >= 0)
        def _():
            line_copy(at, send(0, d), recv(0, d), z - d, z - 1).wait_recv()

        @pl.when(z + d < n)
        def _():
            line_copy(at, send(1, d), recv(1, d), z + d, z + 1).wait_recv()

    def x_line(s):
        return (
            lambda j: x_all.at[s, j],
            lambda way, d: xs_sem.at[s, way, d - 1],
            lambda way, d: xr_sem.at[s, way, d - 1],
        )

    w_line = (
        lambda j: wo.at[j],
        lambda way, d: ws_sem.at[way, d - 1],
        lambda way, d: wr_sem.at[way, d - 1],
    )

    def route(s, r):
        if r % 2:
            return flip(b, r - 1, nb), flip(b, 1, nb), flip(b, r, nb)
        first, second = low_bit(r), high_bit(r)
        odd = s % 2
        blocks = [flip(b, r ^ step, nb) for step in (second, first)]
        peers = [flip(b, step, nb) for step in (second, first)]
        return (
            blocks[0] * (1 - odd) + blocks[1] * odd,
            peers[0] * (1 - odd) + peers[1] * odd,
            flip(b, r, nb),
        )

    def kv_send(s, r):
        block, peer, _ = route(s, r)
        return pltpu.make_async_remote_copy(
            src_ref=kv.at[s, block], dst_ref=kv.at[s, block],
            send_sem=ks_sem.at[s, r], recv_sem=kr_sem.at[s, r],
            device_id={"blk": peer, "head": z}, device_id_type=MESH,
        )

    def kv_recv(s, r):
        _, peer, mine = route(s, r)
        pltpu.make_async_remote_copy(
            src_ref=kv.at[s, mine], dst_ref=kv.at[s, mine],
            send_sem=ks_sem.at[s, r], recv_sem=kr_sem.at[s, r],
            device_id={"blk": peer, "head": z}, device_id_type=MESH,
        ).wait_recv()

    def gated_copy(s, o):
        to = (z + o) % n
        return pltpu.make_async_remote_copy(
            src_ref=gout.at[s, to], dst_ref=gin.at[s, z],
            send_sem=gs_sem.at[s, o], recv_sem=gr_sem.at[s, o],
            device_id={"blk": b, "head": to}, device_id_type=MESH,
        )

    def gated_recv(s, o):
        source = (z + n - o) % n
        pltpu.make_async_remote_copy(
            src_ref=gin.at[s, source], dst_ref=gin.at[s, source],
            send_sem=gs_sem.at[s, o], recv_sem=gr_sem.at[s, o],
            device_id={"blk": b, "head": source}, device_id_type=MESH,
        ).wait_recv()

    rows = lax.broadcasted_iota(jnp.int32, (td, 128), 0)
    lanes = lax.broadcasted_iota(jnp.int32, (td, 128), 1)
    chains = cemb_ref.shape[0]
    chain = jnp.zeros((td, 128), jnp.int32)
    for i in range(td):
        chain = jnp.where(rows == i, chain_ref[i], chain)
    position = (b * n + z) * td + rows
    hot = jnp.zeros((td, 128), jnp.int32)
    for i in range(hot_ref.shape[0]):
        hot = jnp.where(position == hot_ref[i], 1, hot)
    picks = jnp.where(lanes == chain, 1.0, jnp.where(lanes == chains, hot.astype(jnp.float32), 0.0))
    table[...] = jnp.zeros_like(table)
    table[0:chains] = cemb_ref[...].astype(jnp.float32)
    table[chains : chains + 1] = hemb_ref[...].astype(jnp.float32)
    cond[...] = jnp.dot(
        picks.astype(jnp.bfloat16), table[...].astype(jnp.bfloat16), preferred_element_type=jnp.float32
    )

    pl.semaphore_wait(barrier, n - 1 + len(bits))

    def normalize(s, carry):
        shifted = tok_ref[s].astype(jnp.float32) + cond[...]
        average = jnp.mean(shifted, axis=-1, keepdims=True)
        centered = shifted - average
        spread = jnp.mean(centered * centered, axis=-1, keepdims=True)
        x_all[s, z] = (centered * lax.rsqrt(spread + 1e-05)).astype(jnp.bfloat16)
        line_send(*x_line(s), 1, lambda copy: copy.start())
        return carry

    lax.fori_loop(0, samples, normalize, 0)

    wo[z] = wout_ref[...]
    tile = 128 if w_ref.shape[1] % 128 == 0 else w_ref.shape[1]
    for c in range(0, w_ref.shape[1], tile):
        w_t[c : c + tile] = w_ref[:, c : c + tile].astype(jnp.float32).T.astype(jnp.bfloat16)

    evens = [r for r in range(2, nb, 2)]
    levels = max(bin(r).count("1") for r in evens)
    attend_lag = levels + 1
    out_lag = attend_lag + 1

    def at_sample(s, act):
        @pl.when((s >= 0) & (s < samples))
        def _():
            act(s)

    def project(s):
        x = x_all[s].reshape(tb, width)
        proj = lax.dot_general(
            w_t[...], x, (((1,), (1,)), ((), ())), preferred_element_type=jnp.float32
        )
        keys, values = [], []
        for h in range(hh):
            base = h * 4 * HD
            keys.append(proj[base + HD : base + 2 * HD])
            values.append(proj[base + 2 * HD : base + 3 * HD])
        kv[s, b] = jnp.concatenate(keys + values, axis=0).astype(jnp.bfloat16)
        for bit in bits:
            kv_send(s, bit).start()
        for h in range(hh):
            base = h * 4 * HD
            q_all[s, h] = (proj[base : base + HD] * (1.0 / HD**0.5)).T.astype(jnp.bfloat16)
            gate_all[s, h] = jax.nn.sigmoid(proj[base + 3 * HD : base + 4 * HD]).T

    def forward(level):
        def act(s):
            for r in evens:
                if bin(r).count("1") != level:
                    continue
                kv_recv(s, r)
                kv_send(s, r + 1).start()
                for bit in bits[1:]:
                    if r & bit:
                        continue
                    later = r | bit
                    first, second = low_bit(later), high_bit(later)
                    if bit == second:

                        @pl.when(s % 2 == 0)
                        def _(later=later):
                            kv_send(s, later).start()

                    if bit == first:

                        @pl.when(s % 2 == 1)
                        def _(later=later):
                            kv_send(s, later).start()

        return act

    def attend(s):
        for r in range(1, nb, 2):
            kv_recv(s, r)
        ones = jnp.ones((16, nb * tb), jnp.bfloat16)
        parts = []
        for h in range(hh):
            key = jnp.concatenate([kv[s, a, h * HD : (h + 1) * HD, :] for a in range(nb)], axis=1)
            value = jnp.concatenate(
                [kv[s, a, cols + h * HD : cols + (h + 1) * HD, :] for a in range(nb)], axis=1
            )
            scores = jnp.dot(q_all[s, h], key, preferred_element_type=jnp.float32)
            scores = scores + bias_ref[h].astype(jnp.float32)
            top = jnp.max(scores, axis=-1, keepdims=True)
            probs = jnp.exp(scores - top).astype(jnp.bfloat16)
            weighted = lax.dot_general(
                probs, jnp.concatenate([value, ones], axis=0), (((1,), (1,)), ((), ())),
                preferred_element_type=jnp.float32,
            )
            parts.append(weighted[:, :HD] / weighted[:, HD : HD + 1] * gate_all[s, h])
        gated = jnp.concatenate(parts, axis=1)
        for j in range(n):
            gout[s, j] = gated[j * td : (j + 1) * td].astype(jnp.bfloat16)
        for o in range(1, n):
            gated_copy(s, o).start()
        gin[s, z] = gout[s, z]

    def project_out(s):
        for o in range(1, n):
            gated_recv(s, o)
        total = jnp.zeros((td, width), jnp.float32)
        for j in range(n):
            total = total + jnp.dot(gin[s, j], wo[j], preferred_element_type=jnp.float32)
        out_ref[s] = total.astype(out_ref.dtype)

    def step(t, carry):
        for d in range(1, n):

            def hop(s, d=d):
                line_recv(*x_line(s), d)
                if d + 1 < n:
                    line_send(*x_line(s), d + 1, lambda copy: copy.start())

            at_sample(t + (n - 1 - d), hop)
        for level in range(1, levels + 1):
            at_sample(t - level, forward(level))
        at_sample(t, project)

        @pl.when(t == 0)
        def _():
            line_send(*w_line, 1, lambda copy: copy.start())

        for d in range(1, n):

            @pl.when(t == min(d + 1, out_lag))
            def _(d=d):
                line_recv(*w_line, d)
                if d + 1 < n:
                    line_send(*w_line, d + 1, lambda copy: copy.start())

        at_sample(t - attend_lag, attend)
        at_sample(t - out_lag, project_out)
        return carry

    lax.fori_loop(-(n - 2), samples + out_lag, step, 0)

    def drain(s, carry):
        for d in range(1, n):
            line_send(*x_line(s), d, lambda copy: copy.wait_send())
        for r in range(1, nb):
            kv_send(s, r).wait_send()
        for o in range(1, n):
            gated_copy(s, o).wait_send()
        return carry

    lax.fori_loop(0, samples, drain, 0)
    for d in range(1, n):
        line_send(*w_line, d, lambda copy: copy.wait_send())


def body(n, nb, tokens, chain_id, hotspots, chain_embed, hot_embed, w_proj, pair_bias, w_out):
    samples, td, width = tokens.shape
    hh, tb, keys = pair_bias.shape
    cols = hh * HD
    smem = pl.BlockSpec(memory_space=pltpu.SMEM)
    vmem = pl.BlockSpec(memory_space=pltpu.VMEM)
    bf16, f32 = jnp.bfloat16, jnp.float32
    dma = pltpu.SemaphoreType.DMA
    return pl.pallas_call(
        functools.partial(kernel, n, nb),
        out_shape=jax.ShapeDtypeStruct((samples, td, width), bf16),
        in_specs=[smem, smem] + [vmem] * 6,
        out_specs=vmem,
        scratch_shapes=[
            pltpu.VMEM((samples, n, td, width), bf16),
            pltpu.VMEM((128, width), f32),
            pltpu.VMEM((td, width), f32),
            pltpu.VMEM((w_proj.shape[1], width), bf16),
            pltpu.VMEM((samples, nb, 2 * cols, tb), bf16),
            pltpu.VMEM((samples, hh, tb, HD), bf16),
            pltpu.VMEM((samples, hh, tb, HD), f32),
            pltpu.VMEM((samples, n, td, cols), bf16),
            pltpu.VMEM((samples, n, td, cols), bf16),
            pltpu.VMEM((n, cols, width), bf16),
            dma((samples, 2, n - 1)),
            dma((samples, 2, n - 1)),
            dma((2, n - 1)),
            dma((2, n - 1)),
            dma((samples, nb)),
            dma((samples, nb)),
            dma((samples, n)),
            dma((samples, n)),
        ],
        compiler_params=pltpu.CompilerParams(
            collective_id=0, has_side_effects=True, vmem_limit_bytes=56 * 1024 * 1024
        ),
    )(chain_id, hotspots, tokens, chain_embed, hot_embed.reshape(1, width), w_proj, pair_bias, w_out)


def solution(mesh):
    in_specs = (
        P(None, ("blk", "head"), None),
        P(("blk", "head")),
        P(),
        P(),
        P(),
        P(None, "head"),
        P("head", "blk", None),
        P("head", None),
    )
    out_specs = P(None, ("blk", "head"), None)
    run = functools.partial(body, mesh.shape["head"], mesh.shape["blk"])
    return jax.shard_map(run, mesh=mesh, in_specs=in_specs, out_specs=out_specs, check_vma=False)
```

```python
import functools
import jax
import jax.numpy as jnp
from jax import lax
from jax.experimental import pallas as pl
from jax.experimental.pallas import tpu as pltpu
from jax.sharding import PartitionSpec as P

HD = 48
LOG2E = 1.4426950408889634
MESH = pl.DeviceIdType.MESH


def flip(index, bits, count):
    total = 0
    weight = 1
    while weight < count:
        bit = (index // weight) % 2
        total = total + ((1 - bit) if (bits // weight) % 2 else bit) * weight
        weight *= 2
    return total


def low_bit(r):
    return r & -r


def high_bit(r):
    return 1 << (r.bit_length() - 1)


def kernel(
    n, nb, chain_ref, hot_ref, tok_ref, cemb_ref, hemb_ref, w_ref, bias_ref, wout_ref, out_ref,
    x_all, table, cond, w_v, w_t, bias_v, bias_f, sc, kv, q_all, gate_all, gout, gin, wo, local_sem,
    xs_sem, xr_sem, ws_sem, wr_sem, ks_sem, kr_sem, gs_sem, gr_sem,
):
    samples, td, width = tok_ref.shape
    hh = bias_ref.shape[0]
    tb = n * td
    cols = hh * HD
    z = lax.axis_index("head")
    b = lax.axis_index("blk")
    bits = [1 << k for k in range(nb.bit_length() - 1)]

    w_copy = pltpu.make_async_copy(w_ref, w_v, local_sem.at[0])
    wo_copy = pltpu.make_async_copy(wout_ref, wo.at[z], local_sem.at[1])
    bias_copy = pltpu.make_async_copy(bias_ref, bias_v, local_sem.at[2])
    barrier = pltpu.get_barrier_semaphore()
    for o in range(1, n):
        pl.semaphore_signal(
            barrier, inc=1, device_id={"blk": b, "head": (z + o) % n}, device_id_type=MESH
        )
    for bit in bits:
        pl.semaphore_signal(
            barrier, inc=1, device_id={"blk": flip(b, bit, nb), "head": z}, device_id_type=MESH
        )

    w_copy.start()
    bias_copy.start()
    wo_copy.start()

    def line_copy(at, send, recv, block, to):
        return pltpu.make_async_remote_copy(
            src_ref=at(block), dst_ref=at(block), send_sem=send, recv_sem=recv,
            device_id={"blk": b, "head": to}, device_id_type=MESH,
        )

    def line_send(at, send, recv, d, act):
        @pl.when((z - d + 1 >= 0) & (z + 1 < n))
        def _():
            act(line_copy(at, send(0, d), recv(0, d), z - d + 1, z + 1))

        @pl.when((z + d - 1 < n) & (z >= 1))
        def _():
            act(line_copy(at, send(1, d), recv(1, d), z + d - 1, z - 1))

    def line_recv(at, send, recv, d):
        @pl.when(z - d >= 0)
        def _():
            line_copy(at, send(0, d), recv(0, d), z - d, z - 1).wait_recv()

        @pl.when(z + d < n)
        def _():
            line_copy(at, send(1, d), recv(1, d), z + d, z + 1).wait_recv()

    def x_line(s):
        return (
            lambda j: x_all.at[s, j],
            lambda way, d: xs_sem.at[s, way, d - 1],
            lambda way, d: xr_sem.at[s, way, d - 1],
        )

    w_line = (
        lambda j: wo.at[j],
        lambda way, d: ws_sem.at[way, d - 1],
        lambda way, d: wr_sem.at[way, d - 1],
    )

    def route(s, r):
        if r % 2:
            return flip(b, r - 1, nb), flip(b, 1, nb), flip(b, r, nb)
        first, second = low_bit(r), high_bit(r)
        odd = s % 2
        blocks = [flip(b, r ^ step, nb) for step in (second, first)]
        peers = [flip(b, step, nb) for step in (second, first)]
        return (
            blocks[0] * (1 - odd) + blocks[1] * odd,
            peers[0] * (1 - odd) + peers[1] * odd,
            flip(b, r, nb),
        )

    def kv_send(s, r):
        block, peer, _ = route(s, r)
        return pltpu.make_async_remote_copy(
            src_ref=kv.at[s, block], dst_ref=kv.at[s, block],
            send_sem=ks_sem.at[s, r], recv_sem=kr_sem.at[s, r],
            device_id={"blk": peer, "head": z}, device_id_type=MESH,
        )

    def kv_recv(s, r):
        _, peer, mine = route(s, r)
        pltpu.make_async_remote_copy(
            src_ref=kv.at[s, mine], dst_ref=kv.at[s, mine],
            send_sem=ks_sem.at[s, r], recv_sem=kr_sem.at[s, r],
            device_id={"blk": peer, "head": z}, device_id_type=MESH,
        ).wait_recv()

    def gated_copy(s, o):
        to = (z + o) % n
        return pltpu.make_async_remote_copy(
            src_ref=gout.at[s, to], dst_ref=gin.at[s, z],
            send_sem=gs_sem.at[s, o], recv_sem=gr_sem.at[s, o],
            device_id={"blk": b, "head": to}, device_id_type=MESH,
        )

    def gated_recv(s, o):
        source = (z + n - o) % n
        pltpu.make_async_remote_copy(
            src_ref=gin.at[s, source], dst_ref=gin.at[s, source],
            send_sem=gs_sem.at[s, o], recv_sem=gr_sem.at[s, o],
            device_id={"blk": b, "head": source}, device_id_type=MESH,
        ).wait_recv()

    rows = lax.broadcasted_iota(jnp.int32, (td, 128), 0)
    lanes = lax.broadcasted_iota(jnp.int32, (td, 128), 1)
    chains = cemb_ref.shape[0]
    chain = jnp.zeros((td, 128), jnp.int32)
    for i in range(td):
        chain = jnp.where(rows == i, chain_ref[i], chain)
    position = (b * n + z) * td + rows
    hot = jnp.zeros((td, 128), jnp.int32)
    for i in range(hot_ref.shape[0]):
        hot = jnp.where(position == hot_ref[i], 1, hot)
    picks = jnp.where(lanes == chain, 1.0, jnp.where(lanes == chains, hot.astype(jnp.float32), 0.0))
    table[...] = jnp.zeros_like(table)
    table[0:chains] = cemb_ref[...].astype(jnp.float32)
    table[chains : chains + 1] = hemb_ref[...].astype(jnp.float32).reshape(1, width)
    cond[...] = jnp.dot(
        picks.astype(jnp.bfloat16), table[...].astype(jnp.bfloat16), preferred_element_type=jnp.float32
    )

    pl.semaphore_wait(barrier, n - 1 + len(bits))

    def normalize(s, carry):
        shifted = tok_ref[s].astype(jnp.float32) + cond[...]
        average = jnp.mean(shifted, axis=-1, keepdims=True)
        centered = shifted - average
        spread = jnp.mean(centered * centered, axis=-1, keepdims=True)
        x_all[s, z] = (centered * lax.rsqrt(spread + 1e-05)).astype(jnp.bfloat16)
        line_send(*x_line(s), 1, lambda copy: copy.start())
        return carry

    lax.fori_loop(0, samples, normalize, 0)

    w_copy.wait()
    tile = 128 if w_ref.shape[1] % 128 == 0 else w_ref.shape[1]
    for c in range(0, w_ref.shape[1], tile):
        w_t[c : c + tile] = w_v[:, c : c + tile].astype(jnp.float32).T.astype(jnp.bfloat16)

    evens = [r for r in range(2, nb, 2)]
    levels = max(bin(r).count("1") for r in evens)
    attend_lag = levels + 1
    out_lag = attend_lag + 1

    per = 2
    chunks = nb // per

    def at_sample(s, act):
        @pl.when((s >= 0) & (s < samples))
        def _():
            act(s)

    def project(s):
        x = x_all[s].reshape(tb, width)
        proj = lax.dot_general(
            w_t[...], x, (((1,), (1,)), ((), ())), preferred_element_type=jnp.float32
        )
        keys, values = [], []
        for h in range(hh):
            base = h * 4 * HD
            keys.append(proj[base + HD : base + 2 * HD])
            values.append(proj[base + 2 * HD : base + 3 * HD])
        kv[s, b] = jnp.concatenate(keys + values, axis=0).astype(jnp.bfloat16)
        for bit in bits:
            kv_send(s, bit).start()
        for h in range(hh):
            base = h * 4 * HD
            q_all[s, h] = (proj[base : base + HD] * (LOG2E / HD**0.5)).T.astype(jnp.bfloat16)
            gate_all[s, h] = jax.nn.sigmoid(proj[base + 3 * HD : base + 4 * HD]).T

    def forward(level):
        def act(s):
            for r in evens:
                if bin(r).count("1") != level:
                    continue
                kv_recv(s, r)
                kv_send(s, r + 1).start()
                for bit in bits[1:]:
                    if r & bit:
                        continue
                    later = r | bit
                    first, second = low_bit(later), high_bit(later)
                    if bit == second:

                        @pl.when(s % 2 == 0)
                        def _(later=later):
                            kv_send(s, later).start()

                    if bit == first:

                        @pl.when(s % 2 == 1)
                        def _(later=later):
                            kv_send(s, later).start()

        return act

    def attend(s):
        for r in range(1, nb, 2):
            kv_recv(s, r)
        ones = jnp.ones((16, per * tb), jnp.bfloat16)

        def chunk(h, c, first):
            base = first + h * HD
            blocks = [kv[s, a, base : base + HD, :] for a in range(c * per, (c + 1) * per)]
            return jnp.concatenate(blocks, axis=1)

        def score(h, c):
            here = slice(c * per * tb, (c + 1) * per * tb)
            part = jnp.dot(q_all[s, h], chunk(h, c, 0), preferred_element_type=jnp.float32)
            part = part + bias_f[h, :, here]
            sc[h % 2, :, here] = part
            top = part[:, :tb]
            for i in range(1, per):
                top = jnp.maximum(top, part[:, i * tb : (i + 1) * tb])
            return top

        def weigh(h, c, top):
            here = slice(c * per * tb, (c + 1) * per * tb)
            probs = jnp.exp2((sc[h % 2, :, here] - top).astype(jnp.bfloat16))
            return lax.dot_general(
                probs, jnp.concatenate([chunk(h, c, cols), ones], axis=0), (((1,), (1,)), ((), ())),
                preferred_element_type=jnp.float32,
            )

        parts = []
        tops = [score(0, c) for c in range(chunks)]
        for h in range(hh):
            top = jnp.max(functools.reduce(jnp.maximum, tops), axis=-1, keepdims=True)
            tops, weighted = [], None
            for c in range(chunks):
                if h + 1 < hh:
                    tops.append(score(h + 1, c))
                part = weigh(h, c, top)
                weighted = part if weighted is None else weighted + part
            parts.append(weighted[:, :HD] / weighted[:, HD : HD + 1] * gate_all[s, h])
        gated = jnp.concatenate(parts, axis=1)
        for j in range(n):
            gout[s, j] = gated[j * td : (j + 1) * td].astype(jnp.bfloat16)
        for o in range(1, n):
            gated_copy(s, o).start()
        gin[s, z] = gout[s, z]

    def project_out(s):
        for o in range(1, n):
            gated_recv(s, o)

        @pl.when(s % 2 == 1)
        def _():
            total = jnp.zeros((2 * td, width), jnp.float32)
            for j in range(n):
                pair = gin[pl.ds(s - 1, 2), j].reshape(2 * td, cols)
                total = total + jnp.dot(pair, wo[j], preferred_element_type=jnp.float32)
            out_ref[pl.ds(s - 1, 2)] = total.reshape(2, td, width).astype(out_ref.dtype)

    def step(t, carry):
        for d in range(1, n):

            def hop(s, d=d):
                line_recv(*x_line(s), d)
                if d + 1 < n:
                    line_send(*x_line(s), d + 1, lambda copy: copy.start())

            at_sample(t + (n - 1 - d), hop)
        for level in range(1, levels + 1):
            at_sample(t - level, forward(level))
        at_sample(t, project)

        @pl.when(t == 1)
        def _():
            wo_copy.wait()
            bias_copy.wait()
            for h in range(hh):
                bias_f[h] = bias_v[h].astype(jnp.float32) * LOG2E
            line_send(*w_line, 1, lambda copy: copy.start())

        for d in range(1, n):

            @pl.when(t == min(d + 2, out_lag + 1))
            def _(d=d):
                line_recv(*w_line, d)
                if d + 1 < n:
                    line_send(*w_line, d + 1, lambda copy: copy.start())

        at_sample(t - attend_lag, attend)
        at_sample(t - out_lag, project_out)
        return carry

    lax.fori_loop(-(n - 2), samples + out_lag, step, 0)

    def drain(s, carry):
        for d in range(1, n):
            line_send(*x_line(s), d, lambda copy: copy.wait_send())
        for r in range(1, nb):
            kv_send(s, r).wait_send()
        for o in range(1, n):
            gated_copy(s, o).wait_send()
        return carry

    lax.fori_loop(0, samples, drain, 0)
    for d in range(1, n):
        line_send(*w_line, d, lambda copy: copy.wait_send())


def body(n, nb, tokens, chain_id, hotspots, chain_embed, hot_embed, w_proj, pair_bias, w_out):
    samples, td, width = tokens.shape
    hh, tb, keys = pair_bias.shape
    cols = hh * HD
    smem = pl.BlockSpec(memory_space=pltpu.SMEM)
    vmem = pl.BlockSpec(memory_space=pltpu.VMEM)
    bf16, f32 = jnp.bfloat16, jnp.float32
    dma = pltpu.SemaphoreType.DMA
    return pl.pallas_call(
        functools.partial(kernel, n, nb),
        out_shape=jax.ShapeDtypeStruct((samples, td, width), bf16),
        in_specs=[smem, smem] + [vmem] * 3 + [pl.BlockSpec(memory_space=pl.ANY)] * 3,
        out_specs=vmem,
        scratch_shapes=[
            pltpu.VMEM((samples, n, td, width), bf16),
            pltpu.VMEM((128, width), f32),
            pltpu.VMEM((td, width), f32),
            pltpu.VMEM(w_proj.shape, bf16),
            pltpu.VMEM((w_proj.shape[1], width), bf16),
            pltpu.VMEM(pair_bias.shape, bf16),
            pltpu.VMEM(pair_bias.shape, f32),
            pltpu.VMEM((2, tb, keys), f32),
            pltpu.VMEM((samples, nb, 2 * cols, tb), bf16),
            pltpu.VMEM((samples, hh, tb, HD), bf16),
            pltpu.VMEM((samples, hh, tb, HD), f32),
            pltpu.VMEM((samples, n, td, cols), bf16),
            pltpu.VMEM((samples, n, td, cols), bf16),
            pltpu.VMEM((n, cols, width), bf16),
            dma((3,)),
            dma((samples, 2, n - 1)),
            dma((samples, 2, n - 1)),
            dma((2, n - 1)),
            dma((2, n - 1)),
            dma((samples, nb)),
            dma((samples, nb)),
            dma((samples, n)),
            dma((samples, n)),
        ],
        compiler_params=pltpu.CompilerParams(
            collective_id=0, has_side_effects=True, vmem_limit_bytes=56 * 1024 * 1024
        ),
    )(chain_id, hotspots, tokens, chain_embed, hot_embed, w_proj, pair_bias, w_out)


def solution(mesh):
    in_specs = (
        P(None, ("blk", "head"), None),
        P(("blk", "head")),
        P(),
        P(),
        P(),
        P(None, "head"),
        P("head", "blk", None),
        P("head", None),
    )
    out_specs = P(None, ("blk", "head"), None)
    run = functools.partial(body, mesh.shape["head"], mesh.shape["blk"])
    return jax.shard_map(run, mesh=mesh, in_specs=in_specs, out_specs=out_specs, check_vma=False)
```

```python
import functools
import jax
import jax.numpy as jnp
from jax import lax
from jax.experimental import pallas as pl
from jax.experimental.pallas import tpu as pltpu
from jax.sharding import PartitionSpec as P

HD = 48
LOG2E = 1.4426950408889634
MESH = pl.DeviceIdType.MESH


def flip(index, bits, count):
    total = 0
    weight = 1
    while weight < count:
        bit = (index // weight) % 2
        total = total + ((1 - bit) if (bits // weight) % 2 else bit) * weight
        weight *= 2
    return total


def low_bit(r):
    return r & -r


def high_bit(r):
    return 1 << (r.bit_length() - 1)


def kernel(
    n, nb, chain_ref, hot_ref, tok_ref, cemb_ref, hemb_ref, w_ref, bias_ref, out_ref,
    x_all, table, cond, w_v, w_t, bias_v, bias_f, sc, kv, q_all, gate_all, gout, gin, local_sem,
    xs_sem, xr_sem, ks_sem, kr_sem, gs_sem, gr_sem,
):
    samples, td, width = tok_ref.shape
    hh = bias_ref.shape[0]
    tb = n * td
    cols = hh * HD
    z = lax.axis_index("head")
    b = lax.axis_index("blk")
    bits = [1 << k for k in range(nb.bit_length() - 1)]

    w_copy = pltpu.make_async_copy(w_ref, w_v, local_sem.at[0])
    bias_copy = pltpu.make_async_copy(bias_ref, bias_v, local_sem.at[1])
    barrier = pltpu.get_barrier_semaphore()
    for o in range(1, n):
        pl.semaphore_signal(
            barrier, inc=1, device_id={"blk": b, "head": (z + o) % n}, device_id_type=MESH
        )
    for bit in bits:
        pl.semaphore_signal(
            barrier, inc=1, device_id={"blk": flip(b, bit, nb), "head": z}, device_id_type=MESH
        )

    w_copy.start()
    bias_copy.start()

    def line_copy(at, send, recv, block, to):
        return pltpu.make_async_remote_copy(
            src_ref=at(block), dst_ref=at(block), send_sem=send, recv_sem=recv,
            device_id={"blk": b, "head": to}, device_id_type=MESH,
        )

    def line_send(at, send, recv, d, act):
        @pl.when((z - d + 1 >= 0) & (z + 1 < n))
        def _():
            act(line_copy(at, send(0, d), recv(0, d), z - d + 1, z + 1))

        @pl.when((z + d - 1 < n) & (z >= 1))
        def _():
            act(line_copy(at, send(1, d), recv(1, d), z + d - 1, z - 1))

    def line_recv(at, send, recv, d):
        @pl.when(z - d >= 0)
        def _():
            line_copy(at, send(0, d), recv(0, d), z - d, z - 1).wait_recv()

        @pl.when(z + d < n)
        def _():
            line_copy(at, send(1, d), recv(1, d), z + d, z + 1).wait_recv()

    def x_line(s):
        return (
            lambda j: x_all.at[s, j],
            lambda way, d: xs_sem.at[s, way, d - 1],
            lambda way, d: xr_sem.at[s, way, d - 1],
        )

    def route(s, r):
        if r % 2:
            return flip(b, r - 1, nb), flip(b, 1, nb), flip(b, r, nb)
        first, second = low_bit(r), high_bit(r)
        odd = s % 2
        blocks = [flip(b, r ^ step, nb) for step in (second, first)]
        peers = [flip(b, step, nb) for step in (second, first)]
        return (
            blocks[0] * (1 - odd) + blocks[1] * odd,
            peers[0] * (1 - odd) + peers[1] * odd,
            flip(b, r, nb),
        )

    def kv_send(s, r):
        block, peer, _ = route(s, r)
        return pltpu.make_async_remote_copy(
            src_ref=kv.at[s, block], dst_ref=kv.at[s, block],
            send_sem=ks_sem.at[s, r], recv_sem=kr_sem.at[s, r],
            device_id={"blk": peer, "head": z}, device_id_type=MESH,
        )

    def kv_recv(s, r):
        _, peer, mine = route(s, r)
        pltpu.make_async_remote_copy(
            src_ref=kv.at[s, mine], dst_ref=kv.at[s, mine],
            send_sem=ks_sem.at[s, r], recv_sem=kr_sem.at[s, r],
            device_id={"blk": peer, "head": z}, device_id_type=MESH,
        ).wait_recv()

    def gated_copy(s, o):
        to = (z + o) % n
        return pltpu.make_async_remote_copy(
            src_ref=gout.at[s, to], dst_ref=gin.at[s, z],
            send_sem=gs_sem.at[s, o], recv_sem=gr_sem.at[s, o],
            device_id={"blk": b, "head": to}, device_id_type=MESH,
        )

    def gated_recv(s, o):
        source = (z + n - o) % n
        pltpu.make_async_remote_copy(
            src_ref=gin.at[s, source], dst_ref=gin.at[s, source],
            send_sem=gs_sem.at[s, o], recv_sem=gr_sem.at[s, o],
            device_id={"blk": b, "head": source}, device_id_type=MESH,
        ).wait_recv()

    rows = lax.broadcasted_iota(jnp.int32, (td, 128), 0)
    lanes = lax.broadcasted_iota(jnp.int32, (td, 128), 1)
    chains = cemb_ref.shape[0]
    chain = jnp.zeros((td, 128), jnp.int32)
    for i in range(td):
        chain = jnp.where(rows == i, chain_ref[i], chain)
    position = (b * n + z) * td + rows
    hot = jnp.zeros((td, 128), jnp.int32)
    for i in range(hot_ref.shape[0]):
        hot = jnp.where(position == hot_ref[i], 1, hot)
    picks = jnp.where(lanes == chain, 1.0, jnp.where(lanes == chains, hot.astype(jnp.float32), 0.0))
    table[...] = jnp.zeros_like(table)
    table[0:chains] = cemb_ref[...].astype(jnp.float32)
    table[chains : chains + 1] = hemb_ref[...].astype(jnp.float32).reshape(1, width)
    cond[...] = jnp.dot(
        picks.astype(jnp.bfloat16), table[...].astype(jnp.bfloat16), preferred_element_type=jnp.float32
    )

    pl.semaphore_wait(barrier, n - 1 + len(bits))

    def normalize(s, carry):
        shifted = tok_ref[s].astype(jnp.float32) + cond[...]
        average = jnp.mean(shifted, axis=-1, keepdims=True)
        centered = shifted - average
        spread = jnp.mean(centered * centered, axis=-1, keepdims=True)
        x_all[s, z] = (centered * lax.rsqrt(spread + 1e-05)).astype(jnp.bfloat16)
        line_send(*x_line(s), 1, lambda copy: copy.start())
        return carry

    lax.fori_loop(0, samples, normalize, 0)

    w_copy.wait()
    tile = 128 if w_ref.shape[1] % 128 == 0 else w_ref.shape[1]
    for c in range(0, w_ref.shape[1], tile):
        w_t[c : c + tile] = w_v[:, c : c + tile].astype(jnp.float32).T.astype(jnp.bfloat16)

    evens = [r for r in range(2, nb, 2)]
    levels = max(bin(r).count("1") for r in evens)
    slack = 2
    attend_lag = slack * levels + 1
    out_lag = attend_lag + 1

    per = 2
    chunks = nb // per

    def at_sample(s, act):
        @pl.when((s >= 0) & (s < samples))
        def _():
            act(s)

    def project(s):
        x = x_all[s].reshape(tb, width)
        proj = lax.dot_general(
            w_t[...], x, (((1,), (1,)), ((), ())), preferred_element_type=jnp.float32
        )
        keys, values = [], []
        for h in range(hh):
            base = h * 4 * HD
            keys.append(proj[base + HD : base + 2 * HD])
            values.append(proj[base + 2 * HD : base + 3 * HD])
        kv[s, b] = jnp.concatenate(keys + values, axis=0).astype(jnp.bfloat16)
        for bit in bits:
            kv_send(s, bit).start()
        for h in range(hh):
            base = h * 4 * HD
            q_all[s, h] = (proj[base : base + HD] * (LOG2E / HD**0.5)).T.astype(jnp.bfloat16)
            gate_all[s, h] = jax.nn.sigmoid(proj[base + 3 * HD : base + 4 * HD]).T

    def forward(level):
        def act(s):
            for r in evens:
                if bin(r).count("1") != level:
                    continue
                kv_recv(s, r)
                kv_send(s, r + 1).start()
                for bit in bits[1:]:
                    if r & bit:
                        continue
                    later = r | bit
                    first, second = low_bit(later), high_bit(later)
                    if bit == second:

                        @pl.when(s % 2 == 0)
                        def _(later=later):
                            kv_send(s, later).start()

                    if bit == first:

                        @pl.when(s % 2 == 1)
                        def _(later=later):
                            kv_send(s, later).start()

        return act

    def attend(s):
        for r in range(1, nb, 2):
            kv_recv(s, r)
        ones = jnp.ones((16, per * tb), jnp.bfloat16)

        def chunk(h, c, first):
            base = first + h * HD
            blocks = [kv[s, a, base : base + HD, :] for a in range(c * per, (c + 1) * per)]
            return jnp.concatenate(blocks, axis=1)

        def score(h, c):
            here = slice(c * per * tb, (c + 1) * per * tb)
            part = jnp.dot(q_all[s, h], chunk(h, c, 0), preferred_element_type=jnp.float32)
            part = part + bias_f[h, :, here]
            sc[h % 2, :, here] = part
            top = part[:, :tb]
            for i in range(1, per):
                top = jnp.maximum(top, part[:, i * tb : (i + 1) * tb])
            return top

        def weigh(h, c, top):
            here = slice(c * per * tb, (c + 1) * per * tb)
            probs = jnp.exp2((sc[h % 2, :, here] - top).astype(jnp.bfloat16))
            return lax.dot_general(
                probs, jnp.concatenate([chunk(h, c, cols), ones], axis=0), (((1,), (1,)), ((), ())),
                preferred_element_type=jnp.float32,
            )

        parts = []
        tops = [score(0, c) for c in range(chunks)]
        for h in range(hh):
            top = jnp.max(functools.reduce(jnp.maximum, tops), axis=-1, keepdims=True)
            tops, weighted = [], None
            for c in range(chunks):
                if h + 1 < hh:
                    tops.append(score(h + 1, c))
                part = weigh(h, c, top)
                weighted = part if weighted is None else weighted + part
            parts.append(weighted[:, :HD] / weighted[:, HD : HD + 1] * gate_all[s, h])
        gated = jnp.concatenate(parts, axis=1)
        for j in range(n):
            gout[s, j] = gated[j * td : (j + 1) * td].astype(jnp.bfloat16)
        for o in range(1, n):
            gated_copy(s, o).start()
        gin[s, z] = gout[s, z]

    def collect(s):
        for o in range(1, n):
            gated_recv(s, o)
        out_ref[s] = gin[s]

    ahead = slack * (n - 2)

    def step(i, carry):
        t = i - ahead
        for d in range(1, n):

            def hop(s, d=d):
                line_recv(*x_line(s), d)
                if d + 1 < n:
                    line_send(*x_line(s), d + 1, lambda copy: copy.start())

            at_sample(t + slack * (n - 1 - d), hop)
        for level in range(1, levels + 1):
            at_sample(t - slack * level, forward(level))
        at_sample(t, project)

        @pl.when(t == 0)
        def _():
            bias_copy.wait()
            for h in range(hh):
                bias_f[h] = bias_v[h].astype(jnp.float32) * LOG2E

        at_sample(t - attend_lag, attend)
        at_sample(t - out_lag, collect)
        return carry

    lax.fori_loop(0, ahead + samples + out_lag, step, 0)

    def drain(s, carry):
        for d in range(1, n):
            line_send(*x_line(s), d, lambda copy: copy.wait_send())
        for r in range(1, nb):
            kv_send(s, r).wait_send()
        for o in range(1, n):
            gated_copy(s, o).wait_send()
        return carry

    lax.fori_loop(0, samples, drain, 0)


def out_kernel(gated_ref, w_ref, out_ref):
    samples, n, td, cols = gated_ref.shape
    width = w_ref.shape[1]
    total = jnp.zeros((samples * td, width), jnp.float32)
    for j in range(n):
        share = gated_ref[:, j].reshape(samples * td, cols)
        total = total + jnp.dot(
            share, w_ref[j * cols : (j + 1) * cols], preferred_element_type=jnp.float32
        )
    out_ref[...] = total.reshape(samples, td, width).astype(out_ref.dtype)


def body(n, nb, tokens, chain_id, hotspots, chain_embed, hot_embed, w_proj, pair_bias, w_out):
    samples, td, width = tokens.shape
    hh, tb, keys = pair_bias.shape
    cols = hh * HD
    smem = pl.BlockSpec(memory_space=pltpu.SMEM)
    vmem = pl.BlockSpec(memory_space=pltpu.VMEM)
    bf16, f32 = jnp.bfloat16, jnp.float32
    dma = pltpu.SemaphoreType.DMA
    w_all = lax.all_gather(w_out, "head", axis=0, tiled=True)
    gated = pl.pallas_call(
        functools.partial(kernel, n, nb),
        out_shape=jax.ShapeDtypeStruct((samples, n, td, cols), bf16),
        in_specs=[smem, smem] + [vmem] * 3 + [pl.BlockSpec(memory_space=pl.ANY)] * 2,
        out_specs=vmem,
        scratch_shapes=[
            pltpu.VMEM((samples, n, td, width), bf16),
            pltpu.VMEM((128, width), f32),
            pltpu.VMEM((td, width), f32),
            pltpu.VMEM(w_proj.shape, bf16),
            pltpu.VMEM((w_proj.shape[1], width), bf16),
            pltpu.VMEM(pair_bias.shape, bf16),
            pltpu.VMEM(pair_bias.shape, f32),
            pltpu.VMEM((2, tb, keys), f32),
            pltpu.VMEM((samples, nb, 2 * cols, tb), bf16),
            pltpu.VMEM((samples, hh, tb, HD), bf16),
            pltpu.VMEM((samples, hh, tb, HD), f32),
            pltpu.VMEM((samples, n, td, cols), bf16),
            pltpu.VMEM((samples, n, td, cols), bf16),
            dma((2,)),
            dma((samples, 2, n - 1)),
            dma((samples, 2, n - 1)),
            dma((samples, nb)),
            dma((samples, nb)),
            dma((samples, n)),
            dma((samples, n)),
        ],
        compiler_params=pltpu.CompilerParams(
            collective_id=0, has_side_effects=True, vmem_limit_bytes=56 * 1024 * 1024
        ),
    )(chain_id, hotspots, tokens, chain_embed, hot_embed, w_proj, pair_bias)
    return pl.pallas_call(
        out_kernel,
        out_shape=jax.ShapeDtypeStruct((samples, td, width), bf16),
        in_specs=[vmem, vmem],
        out_specs=vmem,
        compiler_params=pltpu.CompilerParams(vmem_limit_bytes=32 * 1024 * 1024),
    )(gated, w_all)


def solution(mesh):
    in_specs = (
        P(None, ("blk", "head"), None),
        P(("blk", "head")),
        P(),
        P(),
        P(),
        P(None, "head"),
        P("head", "blk", None),
        P("head", None),
    )
    out_specs = P(None, ("blk", "head"), None)
    run = functools.partial(body, mesh.shape["head"], mesh.shape["blk"])
    return jax.shard_map(run, mesh=mesh, in_specs=in_specs, out_specs=out_specs, check_vma=False)
```

```python
import functools
import jax
import jax.numpy as jnp
from jax import lax
from jax.experimental import pallas as pl
from jax.experimental.pallas import tpu as pltpu
from jax.sharding import PartitionSpec as P

HD = 48
LOG2E = 1.4426950408889634
MESH = pl.DeviceIdType.MESH


def low_bit(r):
    return r & -r


def high_bit(r):
    return 1 << (r.bit_length() - 1)


def kernel(
    n, nb, chain_ref, hot_ref, tok_ref, cemb_ref, hemb_ref, w_ref, bias_ref, wout_ref, out_ref,
    x_all, table, cond, w_v, w_t, bias_v, bias_f, sc, kv, q_all, gate_all, gout, gin, wo, local_sem,
    xs_sem, xr_sem, ws_sem, wr_sem, ts_sem, tr_sem, ks_sem, kr_sem, gs_sem, gr_sem,
):
    samples, td, width = tok_ref.shape
    hh = bias_ref.shape[0]
    tb = n * td
    cols = hh * HD
    z = lax.axis_index("head")
    b = lax.axis_index("blk")
    bits = [1 << k for k in range(nb.bit_length() - 1)]
    digits = [lax.rem(lax.div(b, bit), 2) for bit in bits]
    flipped = [
        sum(((1 - digit) if r & bit else digit) * bit for digit, bit in zip(digits, bits))
        for r in range(nb)
    ]
    ring = [lax.rem(z + o, n) for o in range(n)]
    pieces, _, piece_rows, piece_cols = wo.shape[0], *wo.shape[1:]
    halves = width // piece_cols
    piece = [lax.rem(flipped[r], pieces) for r in range(pieces)]

    w_copy = pltpu.make_async_copy(w_ref, w_v, local_sem.at[0])
    bias_copy = pltpu.make_async_copy(bias_ref, bias_v, local_sem.at[1])
    wo_copies = [
        pltpu.make_async_copy(
            wout_ref.at[
                pl.ds(p // halves * piece_rows, piece_rows), pl.ds(p % halves * piece_cols, piece_cols)
            ],
            wo.at[p, 0],
            local_sem.at[2 + p],
        )
        for p in range(pieces)
    ]
    barrier = pltpu.get_barrier_semaphore()
    for o in range(1, n):
        pl.semaphore_signal(
            barrier, inc=1, device_id={"blk": b, "head": ring[o]}, device_id_type=MESH
        )
    for bit in bits:
        pl.semaphore_signal(
            barrier, inc=1, device_id={"blk": flipped[bit], "head": z}, device_id_type=MESH
        )

    w_copy.start()
    bias_copy.start()
    for copy in wo_copies:
        copy.start()

    def line_copy(at, send, recv, block, to):
        return pltpu.make_async_remote_copy(
            src_ref=at(block, z), dst_ref=at(block, to), send_sem=send, recv_sem=recv,
            device_id={"blk": b, "head": to}, device_id_type=MESH,
        )

    def line_send(at, send, recv, d, act):
        @pl.when((z - d + 1 >= 0) & (z + 1 < n))
        def _():
            act(line_copy(at, send(0, d), recv(0, d), z - d + 1, z + 1))

        @pl.when((z + d - 1 < n) & (z >= 1))
        def _():
            act(line_copy(at, send(1, d), recv(1, d), z + d - 1, z - 1))

    def line_recv(at, send, recv, d):
        @pl.when(z - d >= 0)
        def _():
            line_copy(lambda j, _: at(j, z), send(0, d), recv(0, d), z - d, z - 1).wait_recv()

        @pl.when(z + d < n)
        def _():
            line_copy(lambda j, _: at(j, z), send(1, d), recv(1, d), z + d, z + 1).wait_recv()

    def x_line(s):
        return (
            lambda j, _: x_all.at[s, j],
            lambda way, d: xs_sem.at[s, way, d - 1],
            lambda way, d: xr_sem.at[s, way, d - 1],
        )

    w_line = (
        lambda j, at: wo.at[piece[0], lax.rem(j - at + n, n)],
        lambda way, d: ws_sem.at[way, d - 1],
        lambda way, d: wr_sem.at[way, d - 1],
    )

    def w_tree(r, back):
        step = 1 if r % 2 else low_bit(r)
        held = piece[r if back else r ^ step]
        ref = wo.at[held, pl.ds(1, n - 1)]
        return pltpu.make_async_remote_copy(
            src_ref=ref, dst_ref=ref, send_sem=ts_sem.at[r], recv_sem=tr_sem.at[r],
            device_id={"blk": flipped[step], "head": z}, device_id_type=MESH,
        )

    def route(s, r):
        if r % 2:
            return flipped[r - 1], flipped[1], flipped[r]
        first, second = low_bit(r), high_bit(r)
        odd = lax.rem(s, 2)
        blocks = [flipped[r ^ step] for step in (second, first)]
        peers = [flipped[step] for step in (second, first)]
        return (
            blocks[0] * (1 - odd) + blocks[1] * odd,
            peers[0] * (1 - odd) + peers[1] * odd,
            flipped[r],
        )

    def kv_send(s, r):
        block, peer, _ = route(s, r)
        return pltpu.make_async_remote_copy(
            src_ref=kv.at[s, block], dst_ref=kv.at[s, block],
            send_sem=ks_sem.at[s, r], recv_sem=kr_sem.at[s, r],
            device_id={"blk": peer, "head": z}, device_id_type=MESH,
        )

    def kv_recv(s, r):
        _, peer, mine = route(s, r)
        pltpu.make_async_remote_copy(
            src_ref=kv.at[s, mine], dst_ref=kv.at[s, mine],
            send_sem=ks_sem.at[s, r], recv_sem=kr_sem.at[s, r],
            device_id={"blk": peer, "head": z}, device_id_type=MESH,
        ).wait_recv()

    def gated_copy(s, o):
        to = ring[o]
        return pltpu.make_async_remote_copy(
            src_ref=gout.at[s, to], dst_ref=gin.at[s, z],
            send_sem=gs_sem.at[s, o], recv_sem=gr_sem.at[s, o],
            device_id={"blk": b, "head": to}, device_id_type=MESH,
        )

    def gated_recv(s, o):
        source = ring[n - o]
        pltpu.make_async_remote_copy(
            src_ref=gin.at[s, source], dst_ref=gin.at[s, source],
            send_sem=gs_sem.at[s, o], recv_sem=gr_sem.at[s, o],
            device_id={"blk": b, "head": source}, device_id_type=MESH,
        ).wait_recv()

    rows = lax.broadcasted_iota(jnp.int32, (td, 128), 0)
    lanes = lax.broadcasted_iota(jnp.int32, (td, 128), 1)
    chains = cemb_ref.shape[0]
    chain = jnp.zeros((td, 128), jnp.int32)
    for i in range(td):
        chain = jnp.where(rows == i, chain_ref[i], chain)
    position = (b * n + z) * td + rows
    hot = jnp.zeros((td, 128), jnp.int32)
    for i in range(hot_ref.shape[0]):
        hot = jnp.where(position == hot_ref[i], 1, hot)
    picks = jnp.where(lanes == chain, 1.0, jnp.where(lanes == chains, hot.astype(jnp.float32), 0.0))
    table[...] = jnp.zeros_like(table)
    table[0:chains] = cemb_ref[...].astype(jnp.float32)
    table[chains : chains + 1] = hemb_ref[...].astype(jnp.float32).reshape(1, width)
    cond[...] = jnp.dot(
        picks.astype(jnp.bfloat16), table[...].astype(jnp.bfloat16), preferred_element_type=jnp.float32
    )

    pl.semaphore_wait(barrier, n - 1 + len(bits))

    def normalize(s, carry):
        shifted = tok_ref[s].astype(jnp.float32) + cond[...]
        average = jnp.mean(shifted, axis=-1, keepdims=True)
        centered = shifted - average
        spread = jnp.mean(centered * centered, axis=-1, keepdims=True)
        x_all[s, z] = (centered * lax.rsqrt(spread + 1e-05)).astype(jnp.bfloat16)
        line_send(*x_line(s), 1, lambda copy: copy.start())
        return carry

    lax.fori_loop(0, samples, normalize, 0)

    w_copy.wait()
    tile = 128 if w_ref.shape[1] % 128 == 0 else w_ref.shape[1]
    for c in range(0, w_ref.shape[1], tile):
        w_t[c : c + tile] = w_v[:, c : c + tile].astype(jnp.float32).T.astype(jnp.bfloat16)

    evens = [r for r in range(2, nb, 2)]
    levels = max(bin(r).count("1") for r in evens)
    slack = 2
    attend_lag = slack * levels + 1
    out_lag = attend_lag + 1

    per = 2
    chunks = nb // per

    def at_sample(s, act):
        @pl.when((s >= 0) & (s < samples))
        def _():
            act(s)

    def project(s):
        x = x_all[s].reshape(tb, width)
        proj = lax.dot_general(
            w_t[...], x, (((1,), (1,)), ((), ())), preferred_element_type=jnp.float32
        )
        keys, values = [], []
        for h in range(hh):
            base = h * 4 * HD
            keys.append(proj[base + HD : base + 2 * HD])
            values.append(proj[base + 2 * HD : base + 3 * HD])
        kv[s, b] = jnp.concatenate(keys + values, axis=0).astype(jnp.bfloat16)
        for bit in bits:
            kv_send(s, bit).start()
        for h in range(hh):
            base = h * 4 * HD
            q_all[s, h] = (proj[base : base + HD] * (LOG2E / HD**0.5)).T.astype(jnp.bfloat16)
            gate_all[s, h] = jax.nn.sigmoid(proj[base + 3 * HD : base + 4 * HD]).T

    def forward(level):
        def act(s):
            for r in evens:
                if bin(r).count("1") != level:
                    continue
                kv_recv(s, r)
                kv_send(s, r + 1).start()
                for bit in bits[1:]:
                    if r & bit:
                        continue
                    later = r | bit
                    first, second = low_bit(later), high_bit(later)
                    if bit == second:

                        @pl.when(s % 2 == 0)
                        def _(later=later):
                            kv_send(s, later).start()

                    if bit == first:

                        @pl.when(s % 2 == 1)
                        def _(later=later):
                            kv_send(s, later).start()

        return act

    def attend(s):
        for r in range(1, nb, 2):
            kv_recv(s, r)
        ones = jnp.ones((16, per * tb), jnp.bfloat16)

        def chunk(h, c, first):
            base = first + h * HD
            blocks = [kv[s, a, base : base + HD, :] for a in range(c * per, (c + 1) * per)]
            return jnp.concatenate(blocks, axis=1)

        def score(h, c):
            here = slice(c * per * tb, (c + 1) * per * tb)
            part = jnp.dot(q_all[s, h], chunk(h, c, 0), preferred_element_type=jnp.float32)
            part = part + bias_f[h, :, here]
            sc[h % 2, :, here] = part
            top = part[:, :tb]
            for i in range(1, per):
                top = jnp.maximum(top, part[:, i * tb : (i + 1) * tb])
            return top

        def weigh(h, c, top):
            here = slice(c * per * tb, (c + 1) * per * tb)
            probs = jnp.exp2((sc[h % 2, :, here] - top).astype(jnp.bfloat16))
            return lax.dot_general(
                probs, jnp.concatenate([chunk(h, c, cols), ones], axis=0), (((1,), (1,)), ((), ())),
                preferred_element_type=jnp.float32,
            )

        parts = []
        tops = [score(0, c) for c in range(chunks)]
        for h in range(hh):
            top = jnp.max(functools.reduce(jnp.maximum, tops), axis=-1, keepdims=True)
            tops, weighted = [], None
            for c in range(chunks):
                if h + 1 < hh:
                    tops.append(score(h + 1, c))
                part = weigh(h, c, top)
                weighted = part if weighted is None else weighted + part
            parts.append(weighted[:, :HD] / weighted[:, HD : HD + 1] * gate_all[s, h])
        gated = jnp.concatenate(parts, axis=1)
        for j in range(n):
            gout[s, j] = gated[j * td : (j + 1) * td].astype(jnp.bfloat16)
        for o in range(1, n):
            gated_copy(s, o).start()
        gin[s, z] = gout[s, z]

    def w_forward(level):
        for r in range(2, pieces, 2):
            if bin(r).count("1") != level:
                continue
            w_tree(r, True).wait_recv()
            w_tree(r + 1, False).start()
            for bit in bits[1:]:
                if not r & bit and (r | bit) < pieces and low_bit(r | bit) == bit:
                    w_tree(r | bit, False).start()

    batch = 4 if samples % 4 == 0 else 1

    def collect(s):
        for o in range(1, n):
            gated_recv(s, o)

        @pl.when(s == batch - 1)
        def _():
            for r in range(1, pieces, 2):
                w_tree(r, True).wait_recv()

        @pl.when(lax.rem(s, batch) == batch - 1)
        def _():
            here = pl.ds(s - (batch - 1), batch)
            total = [jnp.zeros((batch * td, piece_cols), jnp.float32) for _ in range(halves)]
            for j in range(n):
                share = gin[here, ring[j]].reshape(batch * td, cols)
                for half in range(halves):
                    rows = [wo[p, j] for p in range(half, pieces, halves)]
                    total[half] = total[half] + jnp.dot(
                        share, jnp.concatenate(rows, axis=0), preferred_element_type=jnp.float32
                    )
            for half in range(halves):
                part = total[half].reshape(batch, td, piece_cols).astype(out_ref.dtype)
                out_ref[here, :, half * piece_cols : (half + 1) * piece_cols] = part

    ahead = slack * (n - 2)

    def step(i, carry):
        t = i - ahead
        for d in range(1, n):

            def hop(s, d=d):
                line_recv(*x_line(s), d)
                if d + 1 < n:
                    line_send(*x_line(s), d + 1, lambda copy: copy.start())

            at_sample(t + slack * (n - 1 - d), hop)
        for level in range(1, levels + 1):
            at_sample(t - slack * level, forward(level))
        at_sample(t, project)

        @pl.when(t == 0)
        def _():
            bias_copy.wait()
            for h in range(hh):
                bias_f[h] = bias_v[h].astype(jnp.float32) * LOG2E
            for copy in wo_copies:
                copy.wait()
            line_send(*w_line, 1, lambda copy: copy.start())

        for d in range(1, n):

            @pl.when(t == min(d, 3))
            def _(d=d):
                line_recv(*w_line, d)
                if d + 1 < n:
                    line_send(*w_line, d + 1, lambda copy: copy.start())
                else:
                    for bit in bits:
                        if bit < pieces:
                            w_tree(bit, False).start()

        for level in range(1, pieces.bit_length() - 1):

            @pl.when(t == min(n - 1, 3) + 2 * level)
            def _(level=level):
                w_forward(level)

        at_sample(t - attend_lag, attend)
        at_sample(t - out_lag, collect)
        return carry

    lax.fori_loop(0, ahead + samples + out_lag, step, 0)

    def drain(s, carry):
        for d in range(1, n):
            line_send(*x_line(s), d, lambda copy: copy.wait_send())
        for r in range(1, nb):
            kv_send(s, r).wait_send()
        for o in range(1, n):
            gated_copy(s, o).wait_send()
        return carry

    lax.fori_loop(0, samples, drain, 0)
    for d in range(1, n):
        line_send(*w_line, d, lambda copy: copy.wait_send())
    for r in range(1, pieces):
        w_tree(r, False).wait_send()


def body(n, nb, tokens, chain_id, hotspots, chain_embed, hot_embed, w_proj, pair_bias, w_out):
    samples, td, width = tokens.shape
    hh, tb, keys = pair_bias.shape
    cols = hh * HD
    smem = pl.BlockSpec(memory_space=pltpu.SMEM)
    vmem = pl.BlockSpec(memory_space=pltpu.VMEM)
    bf16, f32 = jnp.bfloat16, jnp.float32
    dma = pltpu.SemaphoreType.DMA
    pieces, piece_cols = 2 * hh, width // 2
    return pl.pallas_call(
        functools.partial(kernel, n, nb),
        out_shape=jax.ShapeDtypeStruct((samples, td, width), bf16),
        in_specs=[smem, smem] + [vmem] * 3 + [pl.BlockSpec(memory_space=pl.ANY)] * 3,
        out_specs=vmem,
        scratch_shapes=[
            pltpu.VMEM((samples, n, td, width), bf16),
            pltpu.VMEM((128, width), f32),
            pltpu.VMEM((td, width), f32),
            pltpu.VMEM(w_proj.shape, bf16),
            pltpu.VMEM((w_proj.shape[1], width), bf16),
            pltpu.VMEM(pair_bias.shape, bf16),
            pltpu.VMEM(pair_bias.shape, f32),
            pltpu.VMEM((2, tb, keys), f32),
            pltpu.VMEM((samples, nb, 2 * cols, tb), bf16),
            pltpu.VMEM((samples, hh, tb, HD), bf16),
            pltpu.VMEM((samples, hh, tb, HD), f32),
            pltpu.VMEM((samples, n, td, cols), bf16),
            pltpu.VMEM((samples, n, td, cols), bf16),
            pltpu.VMEM((pieces, n, HD, piece_cols), bf16),
            dma((2 + pieces,)),
            dma((samples, 2, n - 1)),
            dma((samples, 2, n - 1)),
            dma((2, n - 1)),
            dma((2, n - 1)),
            dma((pieces,)),
            dma((pieces,)),
            dma((samples, nb)),
            dma((samples, nb)),
            dma((samples, n)),
            dma((samples, n)),
        ],
        compiler_params=pltpu.CompilerParams(
            collective_id=0, has_side_effects=True, vmem_limit_bytes=56 * 1024 * 1024
        ),
    )(chain_id, hotspots, tokens, chain_embed, hot_embed, w_proj, pair_bias, w_out)


def solution(mesh):
    in_specs = (
        P(None, ("blk", "head"), None),
        P(("blk", "head")),
        P(),
        P(),
        P(),
        P(None, "head"),
        P("head", "blk", None),
        P("head", None),
    )
    out_specs = P(None, ("blk", "head"), None)
    run = functools.partial(body, mesh.shape["head"], mesh.shape["blk"])
    return jax.shard_map(run, mesh=mesh, in_specs=in_specs, out_specs=out_specs, check_vma=False)
```

```python
import functools
import jax
import jax.numpy as jnp
from jax import lax
from jax.experimental import pallas as pl
from jax.experimental.pallas import tpu as pltpu
from jax.sharding import PartitionSpec as P

HD = 48
LOG2E = 1.4426950408889634
MESH = pl.DeviceIdType.MESH


def low_bit(r):
    return r & -r


def high_bit(r):
    return 1 << (r.bit_length() - 1)


def kernel(
    n, nb, chain_ref, hot_ref, tok_ref, cemb_ref, hemb_ref, w_ref, bias_ref, wout_ref, out_ref,
    x_all, table, cond, w_v, w_t, bias_v, bias_f, sc, kv, q_all, gate_all, gout, gin, wo, local_sem,
    xs_sem, xr_sem, ws_sem, wr_sem, ts_sem, tr_sem, ks_sem, kr_sem, gs_sem, gr_sem,
):
    samples, td, width = tok_ref.shape
    hh = bias_ref.shape[0]
    tb = n * td
    cols = hh * HD
    z = lax.axis_index("head")
    b = lax.axis_index("blk")
    bits = [1 << k for k in range(nb.bit_length() - 1)]
    digits = [lax.rem(lax.div(b, bit), 2) for bit in bits]
    flipped = [
        sum(((1 - digit) if r & bit else digit) * bit for digit, bit in zip(digits, bits))
        for r in range(nb)
    ]
    ring = [lax.rem(z + o, n) for o in range(n)]
    pieces, _, piece_rows, piece_cols = wo.shape[0], *wo.shape[1:]
    halves = width // piece_cols
    piece = [lax.rem(flipped[r], pieces) for r in range(pieces)]

    w_copy = pltpu.make_async_copy(w_ref, w_v, local_sem.at[0])
    bias_copy = pltpu.make_async_copy(bias_ref, bias_v, local_sem.at[1])
    wo_copies = [
        pltpu.make_async_copy(
            wout_ref.at[
                pl.ds(p // halves * piece_rows, piece_rows), pl.ds(p % halves * piece_cols, piece_cols)
            ],
            wo.at[p, 0],
            local_sem.at[2 + p],
        )
        for p in range(pieces)
    ]
    barrier = pltpu.get_barrier_semaphore()
    for o in range(1, n):
        pl.semaphore_signal(
            barrier, inc=1, device_id={"blk": b, "head": ring[o]}, device_id_type=MESH
        )
    for bit in bits:
        pl.semaphore_signal(
            barrier, inc=1, device_id={"blk": flipped[bit], "head": z}, device_id_type=MESH
        )

    w_copy.start()
    bias_copy.start()
    for copy in wo_copies:
        copy.start()

    def line_copy(at, send, recv, block, to):
        return pltpu.make_async_remote_copy(
            src_ref=at(block, z), dst_ref=at(block, to), send_sem=send, recv_sem=recv,
            device_id={"blk": b, "head": to}, device_id_type=MESH,
        )

    def line_send(at, send, recv, d, act):
        @pl.when((z - d + 1 >= 0) & (z + 1 < n))
        def _():
            act(line_copy(at, send(0, d), recv(0, d), z - d + 1, z + 1))

        @pl.when((z + d - 1 < n) & (z >= 1))
        def _():
            act(line_copy(at, send(1, d), recv(1, d), z + d - 1, z - 1))

    def line_recv(at, send, recv, d):
        @pl.when(z - d >= 0)
        def _():
            line_copy(lambda j, _: at(j, z), send(0, d), recv(0, d), z - d, z - 1).wait_recv()

        @pl.when(z + d < n)
        def _():
            line_copy(lambda j, _: at(j, z), send(1, d), recv(1, d), z + d, z + 1).wait_recv()

    def x_line(s):
        return (
            lambda j, _: x_all.at[s, j],
            lambda way, d: xs_sem.at[s, way, d - 1],
            lambda way, d: xr_sem.at[s, way, d - 1],
        )

    w_line = (
        lambda j, at: wo.at[piece[0], lax.rem(j - at + n, n)],
        lambda way, d: ws_sem.at[way, d - 1],
        lambda way, d: wr_sem.at[way, d - 1],
    )

    def w_tree(r, back):
        step = 1 if r % 2 else low_bit(r)
        held = piece[r if back else r ^ step]
        ref = wo.at[held, pl.ds(1, n - 1)]
        return pltpu.make_async_remote_copy(
            src_ref=ref, dst_ref=ref, send_sem=ts_sem.at[r], recv_sem=tr_sem.at[r],
            device_id={"blk": flipped[step], "head": z}, device_id_type=MESH,
        )

    def route(s, r):
        if r % 2:
            return flipped[r - 1], flipped[1], flipped[r]
        first, second = low_bit(r), high_bit(r)
        odd = lax.rem(s, 2)
        blocks = [flipped[r ^ step] for step in (second, first)]
        peers = [flipped[step] for step in (second, first)]
        return (
            blocks[0] * (1 - odd) + blocks[1] * odd,
            peers[0] * (1 - odd) + peers[1] * odd,
            flipped[r],
        )

    def kv_send(s, r):
        block, peer, _ = route(s, r)
        return pltpu.make_async_remote_copy(
            src_ref=kv.at[s, block], dst_ref=kv.at[s, block],
            send_sem=ks_sem.at[s, r], recv_sem=kr_sem.at[s, r],
            device_id={"blk": peer, "head": z}, device_id_type=MESH,
        )

    def kv_recv(s, r):
        _, peer, mine = route(s, r)
        pltpu.make_async_remote_copy(
            src_ref=kv.at[s, mine], dst_ref=kv.at[s, mine],
            send_sem=ks_sem.at[s, r], recv_sem=kr_sem.at[s, r],
            device_id={"blk": peer, "head": z}, device_id_type=MESH,
        ).wait_recv()

    def gated_copy(s, o):
        to = ring[o]
        return pltpu.make_async_remote_copy(
            src_ref=gout.at[s, to], dst_ref=gin.at[s, z],
            send_sem=gs_sem.at[s, o], recv_sem=gr_sem.at[s, o],
            device_id={"blk": b, "head": to}, device_id_type=MESH,
        )

    def gated_recv(s, o):
        source = ring[n - o]
        pltpu.make_async_remote_copy(
            src_ref=gin.at[s, source], dst_ref=gin.at[s, source],
            send_sem=gs_sem.at[s, o], recv_sem=gr_sem.at[s, o],
            device_id={"blk": b, "head": source}, device_id_type=MESH,
        ).wait_recv()

    rows = lax.broadcasted_iota(jnp.int32, (td, 128), 0)
    lanes = lax.broadcasted_iota(jnp.int32, (td, 128), 1)
    chains = cemb_ref.shape[0]
    chain = jnp.zeros((td, 128), jnp.int32)
    for i in range(td):
        chain = jnp.where(rows == i, chain_ref[i], chain)
    position = (b * n + z) * td + rows
    hot = jnp.zeros((td, 128), jnp.int32)
    for i in range(hot_ref.shape[0]):
        hot = jnp.where(position == hot_ref[i], 1, hot)
    picks = jnp.where(lanes == chain, 1.0, jnp.where(lanes == chains, hot.astype(jnp.float32), 0.0))
    table[...] = jnp.zeros_like(table)
    table[0:chains] = cemb_ref[...].astype(jnp.float32)
    table[chains : chains + 1] = hemb_ref[...].astype(jnp.float32).reshape(1, width)
    cond[...] = jnp.dot(
        picks.astype(jnp.bfloat16), table[...].astype(jnp.bfloat16), preferred_element_type=jnp.float32
    )

    pl.semaphore_wait(barrier, n - 1 + len(bits))

    def normalize(s, carry):
        shifted = tok_ref[s].astype(jnp.float32) + cond[...]
        average = jnp.mean(shifted, axis=-1, keepdims=True)
        centered = shifted - average
        spread = jnp.mean(centered * centered, axis=-1, keepdims=True)
        x_all[s, z] = (centered * lax.rsqrt(spread + 1e-05)).astype(jnp.bfloat16)

        @pl.when(s < early)
        def _():
            line_send(*x_line(s), 1, lambda copy: copy.start())

        return carry

    early = 2

    lax.fori_loop(0, samples, normalize, 0)

    w_copy.wait()
    tile = 128 if w_ref.shape[1] % 128 == 0 else w_ref.shape[1]
    for c in range(0, w_ref.shape[1], tile):
        w_t[c : c + tile] = w_v[:, c : c + tile].astype(jnp.float32).T.astype(jnp.bfloat16)

    evens = [r for r in range(2, nb, 2)]
    levels = max(bin(r).count("1") for r in evens)
    attend_lag = levels + 1
    out_lag = attend_lag + 1

    per = 2
    chunks = nb // per

    def at_sample(s, act):
        @pl.when((s >= 0) & (s < samples))
        def _():
            act(s)

    def project(s):
        x = x_all[s].reshape(tb, width)
        proj = lax.dot_general(
            w_t[...], x, (((1,), (1,)), ((), ())), preferred_element_type=jnp.float32
        )
        keys, values = [], []
        for h in range(hh):
            base = h * 4 * HD
            keys.append(proj[base + HD : base + 2 * HD])
            values.append(proj[base + 2 * HD : base + 3 * HD])
        kv[s, b] = jnp.concatenate(keys + values, axis=0).astype(jnp.bfloat16)
        for bit in bits:
            kv_send(s, bit).start()
        for h in range(hh):
            base = h * 4 * HD
            q_all[s, h] = (proj[base : base + HD] * (LOG2E / HD**0.5)).T.astype(jnp.bfloat16)
            gate_all[s, h] = jax.nn.sigmoid(proj[base + 3 * HD : base + 4 * HD]).T

    def forward(level):
        def act(s):
            for r in evens:
                if bin(r).count("1") != level:
                    continue
                kv_recv(s, r)
                kv_send(s, r + 1).start()
                for bit in bits[1:]:
                    if r & bit:
                        continue
                    later = r | bit
                    first, second = low_bit(later), high_bit(later)
                    if bit == second:

                        @pl.when(s % 2 == 0)
                        def _(later=later):
                            kv_send(s, later).start()

                    if bit == first:

                        @pl.when(s % 2 == 1)
                        def _(later=later):
                            kv_send(s, later).start()

        return act

    def attend(s):
        for r in range(1, nb, 2):
            kv_recv(s, r)
        ones = jnp.ones((16, per * tb), jnp.bfloat16)

        def chunk(h, c, first):
            base = first + h * HD
            blocks = [kv[s, a, base : base + HD, :] for a in range(c * per, (c + 1) * per)]
            return jnp.concatenate(blocks, axis=1)

        def score(h, c):
            here = slice(c * per * tb, (c + 1) * per * tb)
            part = jnp.dot(q_all[s, h], chunk(h, c, 0), preferred_element_type=jnp.float32)
            part = part + bias_f[h, :, here]
            sc[h % 2, :, here] = part
            top = part[:, :tb]
            for i in range(1, per):
                top = jnp.maximum(top, part[:, i * tb : (i + 1) * tb])
            return top

        def weigh(h, c, top):
            here = slice(c * per * tb, (c + 1) * per * tb)
            probs = jnp.exp2((sc[h % 2, :, here] - top).astype(jnp.bfloat16))
            return lax.dot_general(
                probs, jnp.concatenate([chunk(h, c, cols), ones], axis=0), (((1,), (1,)), ((), ())),
                preferred_element_type=jnp.float32,
            )

        parts = []
        tops = [score(0, c) for c in range(chunks)]
        for h in range(hh):
            top = jnp.max(functools.reduce(jnp.maximum, tops), axis=-1, keepdims=True)
            tops, weighted = [], None
            for c in range(chunks):
                if h + 1 < hh:
                    tops.append(score(h + 1, c))
                part = weigh(h, c, top)
                weighted = part if weighted is None else weighted + part
            parts.append(weighted[:, :HD] / weighted[:, HD : HD + 1] * gate_all[s, h])
        gated = jnp.concatenate(parts, axis=1)
        for j in range(n):
            gout[s, j] = gated[j * td : (j + 1) * td].astype(jnp.bfloat16)
        for o in range(1, n):
            gated_copy(s, o).start()
        gin[s, z] = gout[s, z]

    def w_forward(level):
        for r in range(2, pieces, 2):
            if bin(r).count("1") != level:
                continue
            w_tree(r, True).wait_recv()
            w_tree(r + 1, False).start()
            for bit in bits[1:]:
                if not r & bit and (r | bit) < pieces and low_bit(r | bit) == bit:
                    w_tree(r | bit, False).start()

    batch = 4 if samples % 4 == 0 else 1

    def collect(s):
        for o in range(1, n):
            gated_recv(s, o)

        @pl.when(s == batch - 1)
        def _():
            for r in range(1, pieces, 2):
                w_tree(r, True).wait_recv()

        @pl.when(lax.rem(s, batch) == batch - 1)
        def _():
            here = pl.ds(s - (batch - 1), batch)
            total = [jnp.zeros((batch * td, piece_cols), jnp.float32) for _ in range(halves)]
            for j in range(n):
                share = gin[here, ring[j]].reshape(batch * td, cols)
                for half in range(halves):
                    rows = [wo[p, j] for p in range(half, pieces, halves)]
                    total[half] = total[half] + jnp.dot(
                        share, jnp.concatenate(rows, axis=0), preferred_element_type=jnp.float32
                    )
            for half in range(halves):
                part = total[half].reshape(batch, td, piece_cols).astype(out_ref.dtype)
                out_ref[here, :, half * piece_cols : (half + 1) * piece_cols] = part

    ahead = n - 2

    def step(i, carry):
        t = i - ahead
        for d in range(1, n):

            def hop(s, d=d):
                line_recv(*x_line(s), d)
                if d + 1 < n:
                    line_send(*x_line(s), d + 1, lambda copy: copy.start())

            at_sample(t + (n - 1 - d), hop)
        at_sample(t + ahead + early, lambda s: line_send(*x_line(s), 1, lambda copy: copy.start()))
        at_sample(t, project)
        for level in range(1, levels + 1):
            at_sample(t - level, forward(level))

        @pl.when(t == -1)
        def _():
            bias_copy.wait()
            for h in range(hh):
                bias_f[h] = bias_v[h].astype(jnp.float32) * LOG2E
            for copy in wo_copies:
                copy.wait()
            line_send(*w_line, 1, lambda copy: copy.start())

        for d in range(1, n):

            @pl.when(t == min(d, 3) - 1)
            def _(d=d):
                line_recv(*w_line, d)
                if d + 1 < n:
                    line_send(*w_line, d + 1, lambda copy: copy.start())
                else:
                    for bit in bits:
                        if bit < pieces:
                            w_tree(bit, False).start()

        for level in range(1, pieces.bit_length() - 1):

            @pl.when(t == min(n - 1, 3) - 1 + 2 * level)
            def _(level=level):
                w_forward(level)

        at_sample(t - attend_lag, attend)
        at_sample(t - out_lag, collect)
        return carry

    lax.fori_loop(0, ahead + samples + out_lag, step, 0)

    def drain(s, carry):
        for d in range(1, n):
            line_send(*x_line(s), d, lambda copy: copy.wait_send())
        for r in range(1, nb):
            kv_send(s, r).wait_send()
        for o in range(1, n):
            gated_copy(s, o).wait_send()
        return carry

    lax.fori_loop(0, samples, drain, 0)
    for d in range(1, n):
        line_send(*w_line, d, lambda copy: copy.wait_send())
    for r in range(1, pieces):
        w_tree(r, False).wait_send()


def body(n, nb, tokens, chain_id, hotspots, chain_embed, hot_embed, w_proj, pair_bias, w_out):
    samples, td, width = tokens.shape
    hh, tb, keys = pair_bias.shape
    cols = hh * HD
    smem = pl.BlockSpec(memory_space=pltpu.SMEM)
    vmem = pl.BlockSpec(memory_space=pltpu.VMEM)
    bf16, f32 = jnp.bfloat16, jnp.float32
    dma = pltpu.SemaphoreType.DMA
    pieces, piece_cols = 2 * hh, width // 2
    return pl.pallas_call(
        functools.partial(kernel, n, nb),
        out_shape=jax.ShapeDtypeStruct((samples, td, width), bf16),
        in_specs=[smem, smem] + [vmem] * 3 + [pl.BlockSpec(memory_space=pl.ANY)] * 3,
        out_specs=vmem,
        scratch_shapes=[
            pltpu.VMEM((samples, n, td, width), bf16),
            pltpu.VMEM((128, width), f32),
            pltpu.VMEM((td, width), f32),
            pltpu.VMEM(w_proj.shape, bf16),
            pltpu.VMEM((w_proj.shape[1], width), bf16),
            pltpu.VMEM(pair_bias.shape, bf16),
            pltpu.VMEM(pair_bias.shape, f32),
            pltpu.VMEM((2, tb, keys), f32),
            pltpu.VMEM((samples, nb, 2 * cols, tb), bf16),
            pltpu.VMEM((samples, hh, tb, HD), bf16),
            pltpu.VMEM((samples, hh, tb, HD), f32),
            pltpu.VMEM((samples, n, td, cols), bf16),
            pltpu.VMEM((samples, n, td, cols), bf16),
            pltpu.VMEM((pieces, n, HD, piece_cols), bf16),
            dma((2 + pieces,)),
            dma((samples, 2, n - 1)),
            dma((samples, 2, n - 1)),
            dma((2, n - 1)),
            dma((2, n - 1)),
            dma((pieces,)),
            dma((pieces,)),
            dma((samples, nb)),
            dma((samples, nb)),
            dma((samples, n)),
            dma((samples, n)),
        ],
        compiler_params=pltpu.CompilerParams(
            collective_id=0, has_side_effects=True, vmem_limit_bytes=56 * 1024 * 1024
        ),
    )(chain_id, hotspots, tokens, chain_embed, hot_embed, w_proj, pair_bias, w_out)


def solution(mesh):
    in_specs = (
        P(None, ("blk", "head"), None),
        P(("blk", "head")),
        P(),
        P(),
        P(),
        P(None, "head"),
        P("head", "blk", None),
        P("head", None),
    )
    out_specs = P(None, ("blk", "head"), None)
    run = functools.partial(body, mesh.shape["head"], mesh.shape["blk"])
    return jax.shard_map(run, mesh=mesh, in_specs=in_specs, out_specs=out_specs, check_vma=False)
```

```python
import functools
import jax
import jax.numpy as jnp
from jax import lax
from jax.experimental import pallas as pl
from jax.experimental.pallas import tpu as pltpu
from jax.sharding import PartitionSpec as P

HD = 48
LOG2E = 1.4426950408889634
MESH = pl.DeviceIdType.MESH


def low_bit(r):
    return r & -r


def high_bit(r):
    return 1 << (r.bit_length() - 1)


def kernel(
    n, nb, chain_ref, hot_ref, tok_ref, cemb_ref, hemb_ref, w_ref, bias_ref, wout_ref, out_ref,
    x_all, table, cond, w_v, w_t, bias_v, bias_f, sc, kv, q_all, gate_all, gout, gin, wo, local_sem,
    xs_sem, xr_sem, ws_sem, wr_sem, ts_sem, tr_sem, ks_sem, kr_sem, gs_sem, gr_sem,
):
    samples, td, width = tok_ref.shape
    hh = bias_ref.shape[0]
    tb = n * td
    cols = hh * HD
    z = lax.axis_index("head")
    b = lax.axis_index("blk")
    bits = [1 << k for k in range(nb.bit_length() - 1)]
    digits = [lax.rem(lax.div(b, bit), 2) for bit in bits]
    flipped = [
        sum(((1 - digit) if r & bit else digit) * bit for digit, bit in zip(digits, bits))
        for r in range(nb)
    ]
    ring = [lax.rem(z + o, n) for o in range(n)]
    pieces, _, piece_rows, piece_cols = wo.shape[0], *wo.shape[1:]
    halves = width // piece_cols
    piece = [lax.rem(flipped[r], pieces) for r in range(pieces)]

    w_copy = pltpu.make_async_copy(w_ref, w_v, local_sem.at[0])
    bias_copy = pltpu.make_async_copy(bias_ref, bias_v, local_sem.at[1])
    wo_copies = [
        pltpu.make_async_copy(
            wout_ref.at[
                pl.ds(p // halves * piece_rows, piece_rows), pl.ds(p % halves * piece_cols, piece_cols)
            ],
            wo.at[p, 0],
            local_sem.at[2 + p],
        )
        for p in range(pieces)
    ]
    barrier = pltpu.get_barrier_semaphore()
    for o in range(1, n):
        pl.semaphore_signal(
            barrier, inc=1, device_id={"blk": b, "head": ring[o]}, device_id_type=MESH
        )
    for bit in bits:
        pl.semaphore_signal(
            barrier, inc=1, device_id={"blk": flipped[bit], "head": z}, device_id_type=MESH
        )

    w_copy.start()
    bias_copy.start()
    for copy in wo_copies:
        copy.start()

    def line_copy(at, send, recv, block, to):
        return pltpu.make_async_remote_copy(
            src_ref=at(block, z), dst_ref=at(block, to), send_sem=send, recv_sem=recv,
            device_id={"blk": b, "head": to}, device_id_type=MESH,
        )

    def line_send(at, send, recv, d, act):
        @pl.when((z - d + 1 >= 0) & (z + 1 < n))
        def _():
            act(line_copy(at, send(0, d), recv(0, d), z - d + 1, z + 1))

        @pl.when((z + d - 1 < n) & (z >= 1))
        def _():
            act(line_copy(at, send(1, d), recv(1, d), z + d - 1, z - 1))

    def line_recv(at, send, recv, d):
        @pl.when(z - d >= 0)
        def _():
            line_copy(lambda j, _: at(j, z), send(0, d), recv(0, d), z - d, z - 1).wait_recv()

        @pl.when(z + d < n)
        def _():
            line_copy(lambda j, _: at(j, z), send(1, d), recv(1, d), z + d, z + 1).wait_recv()

    def x_line(s):
        return (
            lambda j, _: x_all.at[s, j],
            lambda way, d: xs_sem.at[s, way, d - 1],
            lambda way, d: xr_sem.at[s, way, d - 1],
        )

    w_line = (
        lambda j, at: wo.at[piece[0], lax.rem(j - at + n, n)],
        lambda way, d: ws_sem.at[way, d - 1],
        lambda way, d: wr_sem.at[way, d - 1],
    )

    def w_tree(r, back):
        step = 1 if r % 2 else low_bit(r)
        held = piece[r if back else r ^ step]
        ref = wo.at[held, pl.ds(1, n - 1)]
        return pltpu.make_async_remote_copy(
            src_ref=ref, dst_ref=ref, send_sem=ts_sem.at[r], recv_sem=tr_sem.at[r],
            device_id={"blk": flipped[step], "head": z}, device_id_type=MESH,
        )

    def route(s, r):
        if r % 2:
            return flipped[r - 1], flipped[1], flipped[r]
        first, second = low_bit(r), high_bit(r)
        odd = lax.rem(s, 2)
        blocks = [flipped[r ^ step] for step in (second, first)]
        peers = [flipped[step] for step in (second, first)]
        return (
            blocks[0] * (1 - odd) + blocks[1] * odd,
            peers[0] * (1 - odd) + peers[1] * odd,
            flipped[r],
        )

    def kv_send(s, r):
        block, peer, _ = route(s, r)
        return pltpu.make_async_remote_copy(
            src_ref=kv.at[s, block], dst_ref=kv.at[s, block],
            send_sem=ks_sem.at[s], recv_sem=kr_sem.at[s, 1 if r % 2 else r],
            device_id={"blk": peer, "head": z}, device_id_type=MESH,
        )

    def kv_recv(s, r):
        _, peer, mine = route(s, r)
        pltpu.make_async_remote_copy(
            src_ref=kv.at[s, mine], dst_ref=kv.at[s, mine],
            send_sem=ks_sem.at[s], recv_sem=kr_sem.at[s, 1 if r % 2 else r],
            device_id={"blk": peer, "head": z}, device_id_type=MESH,
        ).wait_recv()

    def gated_copy(s, o):
        to = ring[o]
        return pltpu.make_async_remote_copy(
            src_ref=gout.at[s, to], dst_ref=gin.at[s, z],
            send_sem=gs_sem.at[s], recv_sem=gr_sem.at[s],
            device_id={"blk": b, "head": to}, device_id_type=MESH,
        )

    def whole_copy(ref, send, recv, blk, head):
        return pltpu.make_async_remote_copy(
            src_ref=ref, dst_ref=ref, send_sem=send, recv_sem=recv,
            device_id={"blk": blk, "head": head}, device_id_type=MESH,
        )

    def sibling_recv(s):
        ref = kv.at[s, pl.ds(0, nb // 2)]
        whole_copy(ref, ks_sem.at[s], kr_sem.at[s, 1], flipped[1], z).wait_recv()

    def kv_sent(s):
        ref = kv.at[s, pl.ds(0, nb - 1)]
        whole_copy(ref, ks_sem.at[s], kr_sem.at[s, 1], flipped[1], z).wait_send()

    def gated_recv(s):
        ref = gin.at[s, pl.ds(0, n - 1)]
        whole_copy(ref, gs_sem.at[s], gr_sem.at[s], b, ring[1]).wait_recv()

    def gated_sent(s):
        ref = gout.at[s, pl.ds(0, n - 1)]
        whole_copy(ref, gs_sem.at[s], gr_sem.at[s], b, ring[1]).wait_send()

    rows = lax.broadcasted_iota(jnp.int32, (td, 128), 0)
    lanes = lax.broadcasted_iota(jnp.int32, (td, 128), 1)
    chains = cemb_ref.shape[0]
    chain = jnp.zeros((td, 128), jnp.int32)
    for i in range(td):
        chain = jnp.where(rows == i, chain_ref[i], chain)
    position = (b * n + z) * td + rows
    hot = jnp.zeros((td, 128), jnp.int32)
    for i in range(hot_ref.shape[0]):
        hot = jnp.where(position == hot_ref[i], 1, hot)
    picks = jnp.where(lanes == chain, 1.0, jnp.where(lanes == chains, hot.astype(jnp.float32), 0.0))
    table[...] = jnp.zeros_like(table)
    table[0:chains] = cemb_ref[...].astype(jnp.float32)
    table[chains : chains + 1] = hemb_ref[...].astype(jnp.float32).reshape(1, width)
    cond[...] = jnp.dot(
        picks.astype(jnp.bfloat16), table[...].astype(jnp.bfloat16), preferred_element_type=jnp.float32
    )

    pl.semaphore_wait(barrier, n - 1 + len(bits))

    def normalize(s):
        shifted = tok_ref[s].astype(jnp.float32) + cond[...]
        average = jnp.mean(shifted, axis=-1, keepdims=True)
        centered = shifted - average
        spread = jnp.mean(centered * centered, axis=-1, keepdims=True)
        x_all[s, z] = (centered * lax.rsqrt(spread + 1e-05)).astype(jnp.bfloat16)
        line_send(*x_line(s), 1, lambda copy: copy.start())

    early = min(2, samples)
    normalize(0)
    for copy in wo_copies:
        copy.wait()
    line_send(*w_line, 1, lambda copy: copy.start())
    for s in range(1, early):
        normalize(s)

    w_copy.wait()
    tile = 128 if w_ref.shape[1] % 128 == 0 else w_ref.shape[1]
    for c in range(0, w_ref.shape[1], tile):
        w_t[c : c + tile] = w_v[:, c : c + tile].astype(jnp.float32).T.astype(jnp.bfloat16)

    evens = [r for r in range(2, nb, 2)]
    levels = max(bin(r).count("1") for r in evens)
    attend_lag = levels + 1
    out_lag = attend_lag + 1

    per = 2
    chunks = nb // per

    def at_sample(s, act):
        @pl.when((s >= 0) & (s < samples))
        def _():
            act(s)

    def project(s):
        x = x_all[s].reshape(tb, width)
        proj = lax.dot_general(
            w_t[...], x, (((1,), (1,)), ((), ())), preferred_element_type=jnp.float32
        )
        keys, values = [], []
        for h in range(hh):
            base = h * 4 * HD
            keys.append(proj[base + HD : base + 2 * HD])
            values.append(proj[base + 2 * HD : base + 3 * HD])
        kv[s, b] = jnp.concatenate(keys + values, axis=0).astype(jnp.bfloat16)
        for bit in bits:
            kv_send(s, bit).start()
        for h in range(hh):
            base = h * 4 * HD
            q_all[s, h] = (proj[base : base + HD] * (LOG2E / HD**0.5)).T.astype(jnp.bfloat16)
            gate_all[s, h] = jax.nn.sigmoid(proj[base + 3 * HD : base + 4 * HD]).T

    def forward(level):
        def act(s):
            for r in evens:
                if bin(r).count("1") != level:
                    continue
                kv_recv(s, r)
                kv_send(s, r + 1).start()
                for bit in bits[1:]:
                    if r & bit:
                        continue
                    later = r | bit
                    first, second = low_bit(later), high_bit(later)
                    if bit == second:

                        @pl.when(s % 2 == 0)
                        def _(later=later):
                            kv_send(s, later).start()

                    if bit == first:

                        @pl.when(s % 2 == 1)
                        def _(later=later):
                            kv_send(s, later).start()

        return act

    def attend(s):
        sibling_recv(s)
        ones = jnp.ones((16, per * tb), jnp.bfloat16)

        def chunk(h, c, first):
            base = first + h * HD
            blocks = [kv[s, a, base : base + HD, :] for a in range(c * per, (c + 1) * per)]
            return jnp.concatenate(blocks, axis=1)

        def score(h, c):
            here = slice(c * per * tb, (c + 1) * per * tb)
            part = jnp.dot(q_all[s, h], chunk(h, c, 0), preferred_element_type=jnp.float32)
            part = part + bias_f[h, :, here]
            sc[h % 2, :, here] = part
            top = part[:, :tb]
            for i in range(1, per):
                top = jnp.maximum(top, part[:, i * tb : (i + 1) * tb])
            return top

        def weigh(h, c, top):
            here = slice(c * per * tb, (c + 1) * per * tb)
            probs = jnp.exp2((sc[h % 2, :, here] - top).astype(jnp.bfloat16))
            return lax.dot_general(
                probs, jnp.concatenate([chunk(h, c, cols), ones], axis=0), (((1,), (1,)), ((), ())),
                preferred_element_type=jnp.float32,
            )

        parts = []
        tops = [score(0, c) for c in range(chunks)]
        for h in range(hh):
            top = jnp.max(functools.reduce(jnp.maximum, tops), axis=-1, keepdims=True)
            tops, weighted = [], None
            for c in range(chunks):
                if h + 1 < hh:
                    tops.append(score(h + 1, c))
                part = weigh(h, c, top)
                weighted = part if weighted is None else weighted + part
            parts.append(weighted[:, :HD] / weighted[:, HD : HD + 1] * gate_all[s, h])
        gated = jnp.concatenate(parts, axis=1)
        for j in range(n):
            gout[s, j] = gated[j * td : (j + 1) * td].astype(jnp.bfloat16)
        for o in range(1, n):
            gated_copy(s, o).start()
        gin[s, z] = gout[s, z]

    def w_forward(level):
        for r in range(2, pieces, 2):
            if bin(r).count("1") != level:
                continue
            w_tree(r, True).wait_recv()
            w_tree(r + 1, False).start()
            for bit in bits[1:]:
                if not r & bit and (r | bit) < pieces and low_bit(r | bit) == bit:
                    w_tree(r | bit, False).start()

    batch = 4 if samples % 4 == 0 else 1

    def collect(s):
        gated_recv(s)

        @pl.when(s == batch - 1)
        def _():
            for r in range(1, pieces, 2):
                w_tree(r, True).wait_recv()

        @pl.when(lax.rem(s, batch) == batch - 1)
        def _():
            here = pl.ds(s - (batch - 1), batch)
            total = [jnp.zeros((batch * td, piece_cols), jnp.float32) for _ in range(halves)]
            for j in range(n):
                share = gin[here, ring[j]].reshape(batch * td, cols)
                for half in range(halves):
                    rows = [wo[p, j] for p in range(half, pieces, halves)]
                    total[half] = total[half] + jnp.dot(
                        share, jnp.concatenate(rows, axis=0), preferred_element_type=jnp.float32
                    )
            for half in range(halves):
                part = total[half].reshape(batch, td, piece_cols).astype(out_ref.dtype)
                out_ref[here, :, half * piece_cols : (half + 1) * piece_cols] = part

    def drain(s):
        for d in range(1, n):
            line_send(*x_line(s), d, lambda copy: copy.wait_send())
        kv_sent(s)
        gated_sent(s)

    ahead = n - 2

    def step(i, carry):
        t = i - ahead
        for d in range(1, n):

            def hop(s, d=d):
                line_recv(*x_line(s), d)
                if d + 1 < n:
                    line_send(*x_line(s), d + 1, lambda copy: copy.start())

            at_sample(t + (n - 1 - d), hop)
        at_sample(t + ahead + early, normalize)
        for d in range(1, n):

            @pl.when(t == min(d, ahead + 1) - ahead - 1)
            def _(d=d):
                line_recv(*w_line, d)
                if d + 1 < n:
                    line_send(*w_line, d + 1, lambda copy: copy.start())
                else:
                    for bit in bits:
                        if bit < pieces:
                            w_tree(bit, False).start()

        for level in range(1, pieces.bit_length() - 1):

            @pl.when(t == level)
            def _(level=level):
                w_forward(level)

        at_sample(t, project)
        for level in range(1, levels + 1):
            at_sample(t - level, forward(level))

        @pl.when(t == -1)
        def _():
            bias_copy.wait()
            for h in range(hh):
                bias_f[h] = bias_v[h].astype(jnp.float32) * LOG2E

        at_sample(t - attend_lag, attend)
        at_sample(t - out_lag, collect)
        at_sample(t - out_lag, drain)
        return carry

    lax.fori_loop(0, ahead + samples + out_lag, step, 0)

    for d in range(1, n):
        line_send(*w_line, d, lambda copy: copy.wait_send())
    for r in range(1, pieces):
        w_tree(r, False).wait_send()


def body(n, nb, tokens, chain_id, hotspots, chain_embed, hot_embed, w_proj, pair_bias, w_out):
    samples, td, width = tokens.shape
    hh, tb, keys = pair_bias.shape
    cols = hh * HD
    smem = pl.BlockSpec(memory_space=pltpu.SMEM)
    vmem = pl.BlockSpec(memory_space=pltpu.VMEM)
    bf16, f32 = jnp.bfloat16, jnp.float32
    dma = pltpu.SemaphoreType.DMA
    pieces, piece_cols = 2 * hh, width // 2
    return pl.pallas_call(
        functools.partial(kernel, n, nb),
        out_shape=jax.ShapeDtypeStruct((samples, td, width), bf16),
        in_specs=[smem, smem] + [vmem] * 3 + [pl.BlockSpec(memory_space=pl.ANY)] * 3,
        out_specs=vmem,
        scratch_shapes=[
            pltpu.VMEM((samples, n, td, width), bf16),
            pltpu.VMEM((128, width), f32),
            pltpu.VMEM((td, width), f32),
            pltpu.VMEM(w_proj.shape, bf16),
            pltpu.VMEM((w_proj.shape[1], width), bf16),
            pltpu.VMEM(pair_bias.shape, bf16),
            pltpu.VMEM(pair_bias.shape, f32),
            pltpu.VMEM((2, tb, keys), f32),
            pltpu.VMEM((samples, nb, 2 * cols, tb), bf16),
            pltpu.VMEM((samples, hh, tb, HD), bf16),
            pltpu.VMEM((samples, hh, tb, HD), f32),
            pltpu.VMEM((samples, n, td, cols), bf16),
            pltpu.VMEM((samples, n, td, cols), bf16),
            pltpu.VMEM((pieces, n, HD, piece_cols), bf16),
            dma((2 + pieces,)),
            dma((samples, 2, n - 1)),
            dma((samples, 2, n - 1)),
            dma((2, n - 1)),
            dma((2, n - 1)),
            dma((pieces,)),
            dma((pieces,)),
            dma((samples,)),
            dma((samples, nb)),
            dma((samples,)),
            dma((samples,)),
        ],
        compiler_params=pltpu.CompilerParams(
            collective_id=0, has_side_effects=True, vmem_limit_bytes=56 * 1024 * 1024
        ),
    )(chain_id, hotspots, tokens, chain_embed, hot_embed, w_proj, pair_bias, w_out)


def solution(mesh):
    in_specs = (
        P(None, ("blk", "head"), None),
        P(("blk", "head")),
        P(),
        P(),
        P(),
        P(None, "head"),
        P("head", "blk", None),
        P("head", None),
    )
    out_specs = P(None, ("blk", "head"), None)
    run = functools.partial(body, mesh.shape["head"], mesh.shape["blk"])
    return jax.shard_map(run, mesh=mesh, in_specs=in_specs, out_specs=out_specs, check_vma=False)
```

```python
import functools
import jax
import jax.numpy as jnp
from jax import lax
from jax.experimental import pallas as pl
from jax.experimental.pallas import tpu as pltpu
from jax.sharding import PartitionSpec as P

HD = 48
LOG2E = 1.4426950408889634
MESH = pl.DeviceIdType.MESH


def low_bit(r):
    return r & -r


def high_bit(r):
    return 1 << (r.bit_length() - 1)


def kernel(
    n, nb, chain_ref, hot_ref, tok_ref, cemb_ref, hemb_ref, w_ref, bias_ref, wout_ref, out_ref,
    x_all, table, cond, w_v, w_t, bias_v, bias_f, sc, kv, q_all, gate_all, gout, gin, wo, local_sem,
    xs_sem, xr_sem, ws_sem, wr_sem, ts_sem, tr_sem, ks_sem, kr_sem, gs_sem, gr_sem,
):
    samples, td, width = tok_ref.shape
    hh = bias_ref.shape[0]
    tb = n * td
    cols = hh * HD
    z = lax.axis_index("head")
    b = lax.axis_index("blk")
    bits = [1 << k for k in range(nb.bit_length() - 1)]
    digits = [lax.rem(lax.div(b, bit), 2) for bit in bits]
    flipped = [
        sum(((1 - digit) if r & bit else digit) * bit for digit, bit in zip(digits, bits))
        for r in range(nb)
    ]
    ring = [lax.rem(z + o, n) for o in range(n)]
    pieces, _, piece_rows, piece_cols = wo.shape[0], *wo.shape[1:]
    halves = width // piece_cols
    piece = [lax.rem(flipped[r], pieces) for r in range(pieces)]

    w_copy = pltpu.make_async_copy(w_ref, w_v, local_sem.at[0])
    bias_copy = pltpu.make_async_copy(bias_ref, bias_v, local_sem.at[1])
    wo_copies = [
        pltpu.make_async_copy(
            wout_ref.at[
                pl.ds(p // halves * piece_rows, piece_rows), pl.ds(p % halves * piece_cols, piece_cols)
            ],
            wo.at[p, 0],
            local_sem.at[2 + p],
        )
        for p in range(pieces)
    ]
    barrier = pltpu.get_barrier_semaphore()
    for o in range(1, n):
        pl.semaphore_signal(
            barrier, inc=1, device_id={"blk": b, "head": ring[o]}, device_id_type=MESH
        )
    for bit in bits:
        pl.semaphore_signal(
            barrier, inc=1, device_id={"blk": flipped[bit], "head": z}, device_id_type=MESH
        )

    w_copy.start()
    bias_copy.start()
    for copy in wo_copies:
        copy.start()

    def line_copy(at, send, recv, block, to):
        return pltpu.make_async_remote_copy(
            src_ref=at(block, z), dst_ref=at(block, to), send_sem=send, recv_sem=recv,
            device_id={"blk": b, "head": to}, device_id_type=MESH,
        )

    def line_send(at, send, recv, d, act):
        @pl.when((z - d + 1 >= 0) & (z + 1 < n))
        def _():
            act(line_copy(at, send(0, d), recv(0, d), z - d + 1, z + 1))

        @pl.when((z + d - 1 < n) & (z >= 1))
        def _():
            act(line_copy(at, send(1, d), recv(1, d), z + d - 1, z - 1))

    def line_recv(at, send, recv, d):
        @pl.when(z - d >= 0)
        def _():
            line_copy(lambda j, _: at(j, z), send(0, d), recv(0, d), z - d, z - 1).wait_recv()

        @pl.when(z + d < n)
        def _():
            line_copy(lambda j, _: at(j, z), send(1, d), recv(1, d), z + d, z + 1).wait_recv()

    def x_line(s):
        return (
            lambda j, _: x_all.at[s, j],
            lambda way, d: xs_sem.at[s, way, d - 1],
            lambda way, d: xr_sem.at[s, way, d - 1],
        )

    w_line = (
        lambda j, at: wo.at[piece[0], lax.rem(j - at + n, n)],
        lambda way, d: ws_sem.at[way, d - 1],
        lambda way, d: wr_sem.at[way, d - 1],
    )

    def w_tree(r, back):
        step = 1 if r % 2 else low_bit(r)
        held = piece[r if back else r ^ step]
        ref = wo.at[held, pl.ds(1, n - 1)]
        return pltpu.make_async_remote_copy(
            src_ref=ref, dst_ref=ref, send_sem=ts_sem.at[r], recv_sem=tr_sem.at[r],
            device_id={"blk": flipped[step], "head": z}, device_id_type=MESH,
        )

    def route(s, r):
        if r % 2:
            return flipped[r - 1], flipped[1], flipped[r]
        first, second = low_bit(r), high_bit(r)
        odd = lax.rem(s, 2)
        blocks = [flipped[r ^ step] for step in (second, first)]
        peers = [flipped[step] for step in (second, first)]
        return (
            blocks[0] * (1 - odd) + blocks[1] * odd,
            peers[0] * (1 - odd) + peers[1] * odd,
            flipped[r],
        )

    def kv_send(s, r):
        block, peer, _ = route(s, r)
        return pltpu.make_async_remote_copy(
            src_ref=kv.at[s, block], dst_ref=kv.at[s, block],
            send_sem=ks_sem.at[s], recv_sem=kr_sem.at[s, 1 if r % 2 else r],
            device_id={"blk": peer, "head": z}, device_id_type=MESH,
        )

    def kv_recv(s, r):
        _, peer, mine = route(s, r)
        pltpu.make_async_remote_copy(
            src_ref=kv.at[s, mine], dst_ref=kv.at[s, mine],
            send_sem=ks_sem.at[s], recv_sem=kr_sem.at[s, 1 if r % 2 else r],
            device_id={"blk": peer, "head": z}, device_id_type=MESH,
        ).wait_recv()

    def gated_copy(s, o):
        to = ring[o]
        return pltpu.make_async_remote_copy(
            src_ref=gout.at[s, to], dst_ref=gin.at[s, z],
            send_sem=gs_sem.at[s], recv_sem=gr_sem.at[s],
            device_id={"blk": b, "head": to}, device_id_type=MESH,
        )

    def whole_copy(ref, send, recv, blk, head):
        return pltpu.make_async_remote_copy(
            src_ref=ref, dst_ref=ref, send_sem=send, recv_sem=recv,
            device_id={"blk": blk, "head": head}, device_id_type=MESH,
        )

    def sibling_recv(s):
        ref = kv.at[s, pl.ds(0, nb // 2)]
        whole_copy(ref, ks_sem.at[s], kr_sem.at[s, 1], flipped[1], z).wait_recv()

    def kv_sent(s):
        ref = kv.at[s, pl.ds(0, nb - 1)]
        whole_copy(ref, ks_sem.at[s], kr_sem.at[s, 1], flipped[1], z).wait_send()

    def gated_recv(s):
        ref = gin.at[s, pl.ds(0, n - 1)]
        whole_copy(ref, gs_sem.at[s], gr_sem.at[s], b, ring[1]).wait_recv()

    def gated_sent(s):
        ref = gout.at[s, pl.ds(0, n - 1)]
        whole_copy(ref, gs_sem.at[s], gr_sem.at[s], b, ring[1]).wait_send()

    rows = lax.broadcasted_iota(jnp.int32, (td, 128), 0)
    lanes = lax.broadcasted_iota(jnp.int32, (td, 128), 1)
    chains = cemb_ref.shape[0]
    chain = jnp.zeros((td, 128), jnp.int32)
    for i in range(td):
        chain = jnp.where(rows == i, chain_ref[i], chain)
    position = (b * n + z) * td + rows
    hot = jnp.zeros((td, 128), jnp.int32)
    for i in range(hot_ref.shape[0]):
        hot = jnp.where(position == hot_ref[i], 1, hot)
    picks = jnp.where(lanes == chain, 1.0, jnp.where(lanes == chains, hot.astype(jnp.float32), 0.0))
    table[...] = jnp.zeros_like(table)
    table[0:chains] = cemb_ref[...].astype(jnp.float32)
    table[chains : chains + 1] = hemb_ref[...].astype(jnp.float32).reshape(1, width)
    cond[...] = jnp.dot(
        picks.astype(jnp.bfloat16), table[...].astype(jnp.bfloat16), preferred_element_type=jnp.float32
    )

    pl.semaphore_wait(barrier, n - 1 + len(bits))

    def normalize(s):
        shifted = tok_ref[s].astype(jnp.float32) + cond[...]
        average = jnp.mean(shifted, axis=-1, keepdims=True)
        centered = shifted - average
        spread = jnp.mean(centered * centered, axis=-1, keepdims=True)
        x_all[s, z] = (centered * lax.rsqrt(spread + 1e-05)).astype(jnp.bfloat16)
        line_send(*x_line(s), 1, lambda copy: copy.start())

    early = min(2, samples)
    normalize(0)
    for copy in wo_copies:
        copy.wait()
    line_send(*w_line, 1, lambda copy: copy.start())
    for s in range(1, early):
        normalize(s)

    w_copy.wait()
    tile = 128 if w_ref.shape[1] % 128 == 0 else w_ref.shape[1]
    for c in range(0, w_ref.shape[1], tile):
        w_t[c : c + tile] = w_v[:, c : c + tile].astype(jnp.float32).T.astype(jnp.bfloat16)

    evens = [r for r in range(2, nb, 2)]
    levels = max(bin(r).count("1") for r in evens)
    attend_lag = levels + 1
    out_lag = attend_lag + 1

    per = 2
    chunks = nb // per

    def at_sample(s, act):
        @pl.when((s >= 0) & (s < samples))
        def _():
            act(s)

    def project(s):
        x = x_all[s].reshape(tb, width)
        proj = lax.dot_general(
            w_t[...], x, (((1,), (1,)), ((), ())), preferred_element_type=jnp.float32
        )
        keys, values = [], []
        for h in range(hh):
            base = h * 4 * HD
            keys.append(proj[base + HD : base + 2 * HD])
            values.append(proj[base + 2 * HD : base + 3 * HD])
        kv[s, b] = jnp.concatenate(keys + values, axis=0).astype(jnp.bfloat16)
        for bit in bits:
            kv_send(s, bit).start()
        for h in range(hh):
            base = h * 4 * HD
            q_all[s, h] = (proj[base : base + HD] * (LOG2E / HD**0.5)).T.astype(jnp.bfloat16)
            gate_all[s, h] = jax.nn.sigmoid(proj[base + 3 * HD : base + 4 * HD]).T

    def forward(level):
        def act(s):
            for r in evens:
                if bin(r).count("1") != level:
                    continue
                kv_recv(s, r)
                kv_send(s, r + 1).start()
                for bit in bits[1:]:
                    if r & bit:
                        continue
                    later = r | bit
                    first, second = low_bit(later), high_bit(later)
                    if bit == second:

                        @pl.when(s % 2 == 0)
                        def _(later=later):
                            kv_send(s, later).start()

                    if bit == first:

                        @pl.when(s % 2 == 1)
                        def _(later=later):
                            kv_send(s, later).start()

        return act

    def attend(s):
        sibling_recv(s)
        ones = jnp.ones((16, per * tb), jnp.bfloat16)

        def chunk(h, c, first):
            base = first + h * HD
            blocks = [kv[s, a, base : base + HD, :] for a in range(c * per, (c + 1) * per)]
            return jnp.concatenate(blocks, axis=1)

        def score(h, c):
            here = slice(c * per * tb, (c + 1) * per * tb)
            part = jnp.dot(q_all[s, h], chunk(h, c, 0), preferred_element_type=jnp.float32)
            part = part + bias_f[h, :, here]
            sc[h % 2, :, here] = part
            top = part[:, :tb]
            for i in range(1, per):
                top = jnp.maximum(top, part[:, i * tb : (i + 1) * tb])
            return top

        def weigh(h, c, top):
            here = slice(c * per * tb, (c + 1) * per * tb)
            probs = jnp.exp2((sc[h % 2, :, here] - top).astype(jnp.bfloat16))
            return lax.dot_general(
                probs, jnp.concatenate([chunk(h, c, cols), ones], axis=0), (((1,), (1,)), ((), ())),
                preferred_element_type=jnp.float32,
            )

        parts = []
        tops = [score(0, c) for c in range(chunks)]
        for h in range(hh):
            top = jnp.max(functools.reduce(jnp.maximum, tops), axis=-1, keepdims=True)
            tops, weighted = [], None
            for c in range(chunks):
                if h + 1 < hh:
                    tops.append(score(h + 1, c))
                part = weigh(h, c, top)
                weighted = part if weighted is None else weighted + part
            parts.append(weighted[:, :HD] / weighted[:, HD : HD + 1] * gate_all[s, h])
        gated = jnp.concatenate(parts, axis=1)
        for j in range(n):
            gout[s, j] = gated[j * td : (j + 1) * td].astype(jnp.bfloat16)
        for o in range(1, n):
            gated_copy(s, o).start()
        gin[s, z] = gout[s, z]

    def w_forward(level):
        for r in range(2, pieces, 2):
            if bin(r).count("1") != level:
                continue
            w_tree(r, True).wait_recv()
            w_tree(r + 1, False).start()
            for bit in bits[1:]:
                if not r & bit and (r | bit) < pieces and low_bit(r | bit) == bit:
                    w_tree(r | bit, False).start()

    batch = 4 if samples % 4 == 0 else 1

    def collect(s):
        gated_recv(s)

        @pl.when(s == batch - 1)
        def _():
            for r in range(1, pieces, 2):
                w_tree(r, True).wait_recv()

        @pl.when(lax.rem(s, batch) == batch - 1)
        def _():
            here = pl.ds(s - (batch - 1), batch)
            total = [jnp.zeros((batch * td, piece_cols), jnp.float32) for _ in range(halves)]
            for j in range(n):
                share = gin[here, ring[j]].reshape(batch * td, cols)
                for half in range(halves):
                    rows = [wo[p, j] for p in range(half, pieces, halves)]
                    total[half] = total[half] + jnp.dot(
                        share, jnp.concatenate(rows, axis=0), preferred_element_type=jnp.float32
                    )
            for half in range(halves):
                part = total[half].reshape(batch, td, piece_cols).astype(out_ref.dtype)
                out_ref[here, :, half * piece_cols : (half + 1) * piece_cols] = part

    def drain(s):
        for d in range(1, n):
            line_send(*x_line(s), d, lambda copy: copy.wait_send())
        kv_sent(s)
        gated_sent(s)

    ahead = n - 2

    def step(i, carry):
        t = i - ahead
        for d in range(1, n):

            def hop(s, d=d):
                line_recv(*x_line(s), d)
                if d + 1 < n:
                    line_send(*x_line(s), d + 1, lambda copy: copy.start())

            at_sample(t + (n - 1 - d), hop)
        at_sample(t + ahead + early, normalize)
        for d in range(1, n):

            @pl.when(t == min(d, ahead + 1) - ahead - 1)
            def _(d=d):
                line_recv(*w_line, d)
                if d + 1 < n:
                    line_send(*w_line, d + 1, lambda copy: copy.start())
                else:
                    for bit in bits:
                        if bit < pieces:
                            w_tree(bit, False).start()

        for level in range(1, pieces.bit_length() - 1):

            @pl.when(t == level)
            def _(level=level):
                w_forward(level)

        at_sample(t, project)

        @pl.when(t == -1)
        def _():
            bias_copy.wait()
            for h in range(hh):
                bias_f[h] = bias_v[h].astype(jnp.float32) * LOG2E

        at_sample(t - attend_lag, attend)
        at_sample(t - out_lag, collect)
        for level in range(1, levels + 1):
            at_sample(t - level, forward(level))
        at_sample(t - out_lag, drain)
        return carry

    lax.fori_loop(0, ahead + samples + out_lag, step, 0)

    for d in range(1, n):
        line_send(*w_line, d, lambda copy: copy.wait_send())
    for r in range(1, pieces):
        w_tree(r, False).wait_send()


def body(n, nb, tokens, chain_id, hotspots, chain_embed, hot_embed, w_proj, pair_bias, w_out):
    samples, td, width = tokens.shape
    hh, tb, keys = pair_bias.shape
    cols = hh * HD
    smem = pl.BlockSpec(memory_space=pltpu.SMEM)
    vmem = pl.BlockSpec(memory_space=pltpu.VMEM)
    bf16, f32 = jnp.bfloat16, jnp.float32
    dma = pltpu.SemaphoreType.DMA
    pieces, piece_cols = 2 * hh, width // 2
    return pl.pallas_call(
        functools.partial(kernel, n, nb),
        out_shape=jax.ShapeDtypeStruct((samples, td, width), bf16),
        in_specs=[smem, smem] + [vmem] * 3 + [pl.BlockSpec(memory_space=pl.ANY)] * 3,
        out_specs=vmem,
        scratch_shapes=[
            pltpu.VMEM((samples, n, td, width), bf16),
            pltpu.VMEM((128, width), f32),
            pltpu.VMEM((td, width), f32),
            pltpu.VMEM(w_proj.shape, bf16),
            pltpu.VMEM((w_proj.shape[1], width), bf16),
            pltpu.VMEM(pair_bias.shape, bf16),
            pltpu.VMEM(pair_bias.shape, f32),
            pltpu.VMEM((2, tb, keys), f32),
            pltpu.VMEM((samples, nb, 2 * cols, tb), bf16),
            pltpu.VMEM((samples, hh, tb, HD), bf16),
            pltpu.VMEM((samples, hh, tb, HD), f32),
            pltpu.VMEM((samples, n, td, cols), bf16),
            pltpu.VMEM((samples, n, td, cols), bf16),
            pltpu.VMEM((pieces, n, HD, piece_cols), bf16),
            dma((2 + pieces,)),
            dma((samples, 2, n - 1)),
            dma((samples, 2, n - 1)),
            dma((2, n - 1)),
            dma((2, n - 1)),
            dma((pieces,)),
            dma((pieces,)),
            dma((samples,)),
            dma((samples, nb)),
            dma((samples,)),
            dma((samples,)),
        ],
        compiler_params=pltpu.CompilerParams(
            collective_id=0, has_side_effects=True, vmem_limit_bytes=56 * 1024 * 1024
        ),
    )(chain_id, hotspots, tokens, chain_embed, hot_embed, w_proj, pair_bias, w_out)


def solution(mesh):
    in_specs = (
        P(None, ("blk", "head"), None),
        P(("blk", "head")),
        P(),
        P(),
        P(),
        P(None, "head"),
        P("head", "blk", None),
        P("head", None),
    )
    out_specs = P(None, ("blk", "head"), None)
    run = functools.partial(body, mesh.shape["head"], mesh.shape["blk"])
    return jax.shard_map(run, mesh=mesh, in_specs=in_specs, out_specs=out_specs, check_vma=False)
```

```python
import functools
import jax
import jax.numpy as jnp
from jax import lax
from jax.experimental import pallas as pl
from jax.experimental.pallas import tpu as pltpu
from jax.sharding import PartitionSpec as P

HD = 48
LOG2E = 1.4426950408889634
MESH = pl.DeviceIdType.MESH


def low_bit(r):
    return r & -r


def high_bit(r):
    return 1 << (r.bit_length() - 1)


def kernel(
    n, nb, chain_ref, hot_ref, tok_ref, cemb_ref, hemb_ref, w_ref, bias_ref, wout_ref, out_ref,
    x_all, table, cond, w_v, w_t, bias_v, bias_f, sc, kv, q_all, gate_all, gout, gin, wo, local_sem,
    xs_sem, xr_sem, ws_sem, wr_sem, ts_sem, tr_sem, ks_sem, kr_sem, gs_sem, gr_sem,
):
    samples, td, width = tok_ref.shape
    hh = bias_ref.shape[0]
    tb = n * td
    cols = hh * HD
    z = lax.axis_index("head")
    b = lax.axis_index("blk")
    bits = [1 << k for k in range(nb.bit_length() - 1)]
    digits = [lax.rem(lax.div(b, bit), 2) for bit in bits]
    flipped = [
        sum(((1 - digit) if r & bit else digit) * bit for digit, bit in zip(digits, bits))
        for r in range(nb)
    ]
    ring = [lax.rem(z + o, n) for o in range(n)]
    pieces, _, piece_rows, piece_cols = wo.shape[0], *wo.shape[1:]
    halves = width // piece_cols
    piece = [lax.rem(flipped[r], pieces) for r in range(pieces)]

    w_copy = pltpu.make_async_copy(w_ref, w_v, local_sem.at[0])
    bias_copy = pltpu.make_async_copy(bias_ref, bias_v, local_sem.at[1])
    wo_copies = [
        pltpu.make_async_copy(
            wout_ref.at[
                pl.ds(p // halves * piece_rows, piece_rows), pl.ds(p % halves * piece_cols, piece_cols)
            ],
            wo.at[p, 0],
            local_sem.at[2 + p],
        )
        for p in range(pieces)
    ]
    barrier = pltpu.get_barrier_semaphore()
    for o in range(1, n):
        pl.semaphore_signal(
            barrier, inc=1, device_id={"blk": b, "head": ring[o]}, device_id_type=MESH
        )
    for bit in bits:
        pl.semaphore_signal(
            barrier, inc=1, device_id={"blk": flipped[bit], "head": z}, device_id_type=MESH
        )

    w_copy.start()
    bias_copy.start()
    for copy in wo_copies:
        copy.start()

    def line_copy(at, send, recv, block, to):
        return pltpu.make_async_remote_copy(
            src_ref=at(block, z), dst_ref=at(block, to), send_sem=send, recv_sem=recv,
            device_id={"blk": b, "head": to}, device_id_type=MESH,
        )

    def line_send(at, send, recv, d, act):
        @pl.when((z - d + 1 >= 0) & (z + 1 < n))
        def _():
            act(line_copy(at, send(0, d), recv(0, d), z - d + 1, z + 1))

        @pl.when((z + d - 1 < n) & (z >= 1))
        def _():
            act(line_copy(at, send(1, d), recv(1, d), z + d - 1, z - 1))

    def line_recv(at, send, recv, d):
        @pl.when(z - d >= 0)
        def _():
            line_copy(lambda j, _: at(j, z), send(0, d), recv(0, d), z - d, z - 1).wait_recv()

        @pl.when(z + d < n)
        def _():
            line_copy(lambda j, _: at(j, z), send(1, d), recv(1, d), z + d, z + 1).wait_recv()

    def x_line(s):
        return (
            lambda j, _: x_all.at[s, j],
            lambda way, d: xs_sem.at[s, way, d - 1],
            lambda way, d: xr_sem.at[s, way, d - 1],
        )

    w_line = (
        lambda j, at: wo.at[piece[0], lax.rem(j - at + n, n)],
        lambda way, d: ws_sem.at[way, d - 1],
        lambda way, d: wr_sem.at[way, d - 1],
    )

    def w_tree(r, back):
        step = 1 if r % 2 else low_bit(r)
        held = piece[r if back else r ^ step]
        ref = wo.at[held, pl.ds(1, n - 1)]
        return pltpu.make_async_remote_copy(
            src_ref=ref, dst_ref=ref, send_sem=ts_sem.at[r], recv_sem=tr_sem.at[r],
            device_id={"blk": flipped[step], "head": z}, device_id_type=MESH,
        )

    def route(s, r):
        if r % 2:
            return flipped[r - 1], flipped[1], flipped[r]
        first, second = low_bit(r), high_bit(r)
        odd = lax.rem(s, 2)
        blocks = [flipped[r ^ step] for step in (second, first)]
        peers = [flipped[step] for step in (second, first)]
        return (
            blocks[0] * (1 - odd) + blocks[1] * odd,
            peers[0] * (1 - odd) + peers[1] * odd,
            flipped[r],
        )

    def kv_send(s, r):
        block, peer, _ = route(s, r)
        return pltpu.make_async_remote_copy(
            src_ref=kv.at[s, block], dst_ref=kv.at[s, block],
            send_sem=ks_sem.at[s], recv_sem=kr_sem.at[s, 1 if r % 2 else r],
            device_id={"blk": peer, "head": z}, device_id_type=MESH,
        )

    def kv_recv(s, r):
        _, peer, mine = route(s, r)
        pltpu.make_async_remote_copy(
            src_ref=kv.at[s, mine], dst_ref=kv.at[s, mine],
            send_sem=ks_sem.at[s], recv_sem=kr_sem.at[s, 1 if r % 2 else r],
            device_id={"blk": peer, "head": z}, device_id_type=MESH,
        ).wait_recv()

    def gated_copy(s, o):
        to = ring[o]
        return pltpu.make_async_remote_copy(
            src_ref=gout.at[s, to], dst_ref=gin.at[s, z],
            send_sem=gs_sem.at[s], recv_sem=gr_sem.at[s],
            device_id={"blk": b, "head": to}, device_id_type=MESH,
        )

    def whole_copy(ref, send, recv, blk, head):
        return pltpu.make_async_remote_copy(
            src_ref=ref, dst_ref=ref, send_sem=send, recv_sem=recv,
            device_id={"blk": blk, "head": head}, device_id_type=MESH,
        )

    def sibling_recv(s):
        ref = kv.at[s, pl.ds(0, nb // 2)]
        whole_copy(ref, ks_sem.at[s], kr_sem.at[s, 1], flipped[1], z).wait_recv()

    def kv_sent(s):
        ref = kv.at[s, pl.ds(0, nb - 1)]
        whole_copy(ref, ks_sem.at[s], kr_sem.at[s, 1], flipped[1], z).wait_send()

    def gated_recv(s):
        ref = gin.at[s, pl.ds(0, n - 1)]
        whole_copy(ref, gs_sem.at[s], gr_sem.at[s], b, ring[1]).wait_recv()

    def gated_sent(s):
        ref = gout.at[s, pl.ds(0, n - 1)]
        whole_copy(ref, gs_sem.at[s], gr_sem.at[s], b, ring[1]).wait_send()

    rows = lax.broadcasted_iota(jnp.int32, (td, 128), 0)
    lanes = lax.broadcasted_iota(jnp.int32, (td, 128), 1)
    chains = cemb_ref.shape[0]
    chain = jnp.zeros((td, 128), jnp.int32)
    for i in range(td):
        chain = jnp.where(rows == i, chain_ref[i], chain)
    position = (b * n + z) * td + rows
    hot = jnp.zeros((td, 128), jnp.int32)
    for i in range(hot_ref.shape[0]):
        hot = jnp.where(position == hot_ref[i], 1, hot)
    picks = jnp.where(lanes == chain, 1.0, jnp.where(lanes == chains, hot.astype(jnp.float32), 0.0))
    table[...] = jnp.zeros_like(table)
    table[0:chains] = cemb_ref[...].astype(jnp.float32)
    table[chains : chains + 1] = hemb_ref[...].astype(jnp.float32).reshape(1, width)
    cond[...] = jnp.dot(
        picks.astype(jnp.bfloat16), table[...].astype(jnp.bfloat16), preferred_element_type=jnp.float32
    )

    pl.semaphore_wait(barrier, n - 1 + len(bits))

    def normalize(s):
        shifted = tok_ref[s].astype(jnp.float32) + cond[...]
        average = jnp.mean(shifted, axis=-1, keepdims=True)
        centered = shifted - average
        spread = jnp.mean(centered * centered, axis=-1, keepdims=True)
        x_all[s, z] = (centered * lax.rsqrt(spread + 1e-05)).astype(jnp.bfloat16)
        line_send(*x_line(s), 1, lambda copy: copy.start())

    early = min(2, samples)
    normalize(0)
    for copy in wo_copies:
        copy.wait()
    line_send(*w_line, 1, lambda copy: copy.start())
    for s in range(1, early):
        normalize(s)

    w_copy.wait()
    tile = 128 if w_ref.shape[1] % 128 == 0 else w_ref.shape[1]
    for c in range(0, w_ref.shape[1], tile):
        w_t[c : c + tile] = w_v[:, c : c + tile].astype(jnp.float32).T.astype(jnp.bfloat16)

    evens = [r for r in range(2, nb, 2)]
    levels = max(bin(r).count("1") for r in evens)
    attend_lag = levels + 1
    out_lag = attend_lag + 1

    per = 2
    chunks = nb // per

    def at_sample(s, act):
        @pl.when((s >= 0) & (s < samples))
        def _():
            act(s)

    def project(s):
        x = x_all[s].reshape(tb, width)
        proj = lax.dot_general(
            w_t[...], x, (((1,), (1,)), ((), ())), preferred_element_type=jnp.float32
        )
        keys, values = [], []
        for h in range(hh):
            base = h * 4 * HD
            keys.append(proj[base + HD : base + 2 * HD])
            values.append(proj[base + 2 * HD : base + 3 * HD])
        kv[s, b] = jnp.concatenate(keys + values, axis=0).astype(jnp.bfloat16)
        for bit in bits:
            kv_send(s, bit).start()
        for h in range(hh):
            base = h * 4 * HD
            q_all[s, h] = (proj[base : base + HD] * (LOG2E / HD**0.5)).T.astype(jnp.bfloat16)
            gate_all[s, h] = jax.nn.sigmoid(proj[base + 3 * HD : base + 4 * HD]).T

    def forward(level):
        def act(s):
            for r in evens:
                if bin(r).count("1") != level:
                    continue
                kv_recv(s, r)
                kv_send(s, r + 1).start()
                for bit in bits[1:]:
                    if r & bit:
                        continue
                    later = r | bit
                    first, second = low_bit(later), high_bit(later)
                    if bit == second:

                        @pl.when(s % 2 == 0)
                        def _(later=later):
                            kv_send(s, later).start()

                    if bit == first:

                        @pl.when(s % 2 == 1)
                        def _(later=later):
                            kv_send(s, later).start()

        return act

    def attend(s):
        sibling_recv(s)
        ones = jnp.ones((16, per * tb), jnp.bfloat16)

        def chunk(h, c, first):
            base = first + h * HD
            blocks = [kv[s, a, base : base + HD, :] for a in range(c * per, (c + 1) * per)]
            return jnp.concatenate(blocks, axis=1)

        def score(h, c):
            here = slice(c * per * tb, (c + 1) * per * tb)
            part = jnp.dot(q_all[s, h], chunk(h, c, 0), preferred_element_type=jnp.float32)
            part = part + bias_f[h, :, here]
            sc[h, :, here] = part
            top = part[:, :tb]
            for i in range(1, per):
                top = jnp.maximum(top, part[:, i * tb : (i + 1) * tb])
            return top

        def weigh(h, c, top):
            here = slice(c * per * tb, (c + 1) * per * tb)
            probs = jnp.exp2((sc[h, :, here] - top).astype(jnp.bfloat16))
            return lax.dot_general(
                probs, jnp.concatenate([chunk(h, c, cols), ones], axis=0), (((1,), (1,)), ((), ())),
                preferred_element_type=jnp.float32,
            )

        parts = []
        tops = [[score(h, c) for c in range(chunks)] for h in range(hh)]
        tops = [jnp.max(functools.reduce(jnp.maximum, top), axis=-1, keepdims=True) for top in tops]
        sums = [None] * hh
        for c in range(chunks):
            for h in range(hh):
                part = weigh(h, c, tops[h])
                sums[h] = part if sums[h] is None else sums[h] + part
        for h in range(hh):
            weighted = sums[h]
            parts.append(weighted[:, :HD] / weighted[:, HD : HD + 1] * gate_all[s, h])
        gated = jnp.concatenate(parts, axis=1)
        for j in range(n):
            gout[s, j] = gated[j * td : (j + 1) * td].astype(jnp.bfloat16)
        for o in range(1, n):
            gated_copy(s, o).start()
        gin[s, z] = gout[s, z]

    def w_forward(level):
        for r in range(2, pieces, 2):
            if bin(r).count("1") != level:
                continue
            w_tree(r, True).wait_recv()
            w_tree(r + 1, False).start()
            for bit in bits[1:]:
                if not r & bit and (r | bit) < pieces and low_bit(r | bit) == bit:
                    w_tree(r | bit, False).start()

    batch = 4 if samples % 4 == 0 else 1

    def collect(s):
        gated_recv(s)

        @pl.when(s == batch - 1)
        def _():
            for r in range(1, pieces, 2):
                w_tree(r, True).wait_recv()

        @pl.when(lax.rem(s, batch) == batch - 1)
        def _():
            here = pl.ds(s - (batch - 1), batch)
            total = [jnp.zeros((batch * td, piece_cols), jnp.float32) for _ in range(halves)]
            for j in range(n):
                share = gin[here, ring[j]].reshape(batch * td, cols)
                for half in range(halves):
                    rows = [wo[p, j] for p in range(half, pieces, halves)]
                    total[half] = total[half] + jnp.dot(
                        share, jnp.concatenate(rows, axis=0), preferred_element_type=jnp.float32
                    )
            for half in range(halves):
                part = total[half].reshape(batch, td, piece_cols).astype(out_ref.dtype)
                out_ref[here, :, half * piece_cols : (half + 1) * piece_cols] = part

    def drain(s):
        for d in range(1, n):
            line_send(*x_line(s), d, lambda copy: copy.wait_send())
        kv_sent(s)
        gated_sent(s)

    ahead = n - 2

    def step(i, carry):
        t = i - ahead
        for d in range(1, n):

            def hop(s, d=d):
                line_recv(*x_line(s), d)
                if d + 1 < n:
                    line_send(*x_line(s), d + 1, lambda copy: copy.start())

            at_sample(t + (n - 1 - d), hop)
        at_sample(t + ahead + early, normalize)
        for d in range(1, n):

            @pl.when(t == min(d, ahead + 1) - ahead - 1)
            def _(d=d):
                line_recv(*w_line, d)
                if d + 1 < n:
                    line_send(*w_line, d + 1, lambda copy: copy.start())
                else:
                    for bit in bits:
                        if bit < pieces:
                            w_tree(bit, False).start()

        for level in range(1, pieces.bit_length() - 1):

            @pl.when(t == level)
            def _(level=level):
                w_forward(level)

        at_sample(t, project)

        @pl.when(t == -1)
        def _():
            bias_copy.wait()
            for h in range(hh):
                bias_f[h] = bias_v[h].astype(jnp.float32) * LOG2E

        at_sample(t - attend_lag, attend)
        at_sample(t - out_lag, collect)
        for level in range(1, levels + 1):
            at_sample(t - level, forward(level))
        at_sample(t - out_lag, drain)
        return carry

    lax.fori_loop(0, ahead + samples + out_lag, step, 0)

    for d in range(1, n):
        line_send(*w_line, d, lambda copy: copy.wait_send())
    for r in range(1, pieces):
        w_tree(r, False).wait_send()


def body(n, nb, tokens, chain_id, hotspots, chain_embed, hot_embed, w_proj, pair_bias, w_out):
    samples, td, width = tokens.shape
    hh, tb, keys = pair_bias.shape
    cols = hh * HD
    smem = pl.BlockSpec(memory_space=pltpu.SMEM)
    vmem = pl.BlockSpec(memory_space=pltpu.VMEM)
    bf16, f32 = jnp.bfloat16, jnp.float32
    dma = pltpu.SemaphoreType.DMA
    pieces, piece_cols = 2 * hh, width // 2
    return pl.pallas_call(
        functools.partial(kernel, n, nb),
        out_shape=jax.ShapeDtypeStruct((samples, td, width), bf16),
        in_specs=[smem, smem] + [vmem] * 3 + [pl.BlockSpec(memory_space=pl.ANY)] * 3,
        out_specs=vmem,
        scratch_shapes=[
            pltpu.VMEM((samples, n, td, width), bf16),
            pltpu.VMEM((128, width), f32),
            pltpu.VMEM((td, width), f32),
            pltpu.VMEM(w_proj.shape, bf16),
            pltpu.VMEM((w_proj.shape[1], width), bf16),
            pltpu.VMEM(pair_bias.shape, bf16),
            pltpu.VMEM(pair_bias.shape, f32),
            pltpu.VMEM((hh, tb, keys), f32),
            pltpu.VMEM((samples, nb, 2 * cols, tb), bf16),
            pltpu.VMEM((samples, hh, tb, HD), bf16),
            pltpu.VMEM((samples, hh, tb, HD), f32),
            pltpu.VMEM((samples, n, td, cols), bf16),
            pltpu.VMEM((samples, n, td, cols), bf16),
            pltpu.VMEM((pieces, n, HD, piece_cols), bf16),
            dma((2 + pieces,)),
            dma((samples, 2, n - 1)),
            dma((samples, 2, n - 1)),
            dma((2, n - 1)),
            dma((2, n - 1)),
            dma((pieces,)),
            dma((pieces,)),
            dma((samples,)),
            dma((samples, nb)),
            dma((samples,)),
            dma((samples,)),
        ],
        compiler_params=pltpu.CompilerParams(
            collective_id=0, has_side_effects=True, vmem_limit_bytes=56 * 1024 * 1024
        ),
    )(chain_id, hotspots, tokens, chain_embed, hot_embed, w_proj, pair_bias, w_out)


def solution(mesh):
    in_specs = (
        P(None, ("blk", "head"), None),
        P(("blk", "head")),
        P(),
        P(),
        P(),
        P(None, "head"),
        P("head", "blk", None),
        P("head", None),
    )
    out_specs = P(None, ("blk", "head"), None)
    run = functools.partial(body, mesh.shape["head"], mesh.shape["blk"])
    return jax.shard_map(run, mesh=mesh, in_specs=in_specs, out_specs=out_specs, check_vma=False)
```

```python
import functools
import jax
import jax.numpy as jnp
from jax import lax
from jax.experimental import pallas as pl
from jax.experimental.pallas import tpu as pltpu
from jax.sharding import PartitionSpec as P

HD = 48
LOG2E = 1.4426950408889634
MESH = pl.DeviceIdType.MESH


def low_bit(r):
    return r & -r


def high_bit(r):
    return 1 << (r.bit_length() - 1)


def kernel(
    n, nb, chain_ref, hot_ref, tok_ref, cemb_ref, hemb_ref, w_ref, bias_ref, wout_ref, out_ref,
    x_all, table, cond, w_v, w_t, bias_v, bias_f, sc, kv, q_all, gate_all, gout, gin, wo, local_sem,
    xs_sem, xr_sem, ws_sem, wr_sem, ts_sem, tr_sem, ks_sem, kr_sem, gs_sem, gr_sem,
):
    samples, td, width = tok_ref.shape
    hh = bias_ref.shape[0]
    tb = n * td
    cols = hh * HD
    z = lax.axis_index("head")
    b = lax.axis_index("blk")
    bits = [1 << k for k in range(nb.bit_length() - 1)]
    digits = [lax.rem(lax.div(b, bit), 2) for bit in bits]
    flipped = [
        sum(((1 - digit) if r & bit else digit) * bit for digit, bit in zip(digits, bits))
        for r in range(nb)
    ]
    ring = [lax.rem(z + o, n) for o in range(n)]
    pieces, _, piece_rows, piece_cols = wo.shape[0], *wo.shape[1:]
    halves = width // piece_cols
    piece = [lax.rem(flipped[r], pieces) for r in range(pieces)]

    w_copy = pltpu.make_async_copy(w_ref, w_v, local_sem.at[0])
    bias_copy = pltpu.make_async_copy(bias_ref, bias_v, local_sem.at[1])
    wo_copies = [
        pltpu.make_async_copy(
            wout_ref.at[
                pl.ds(p // halves * piece_rows, piece_rows), pl.ds(p % halves * piece_cols, piece_cols)
            ],
            wo.at[p, 0],
            local_sem.at[2 + p],
        )
        for p in range(pieces)
    ]
    barrier = pltpu.get_barrier_semaphore()
    for o in range(1, n):
        pl.semaphore_signal(
            barrier, inc=1, device_id={"blk": b, "head": ring[o]}, device_id_type=MESH
        )
    for bit in bits:
        pl.semaphore_signal(
            barrier, inc=1, device_id={"blk": flipped[bit], "head": z}, device_id_type=MESH
        )

    w_copy.start()
    bias_copy.start()
    for copy in wo_copies:
        copy.start()

    def line_copy(at, send, recv, block, to):
        return pltpu.make_async_remote_copy(
            src_ref=at(block, z), dst_ref=at(block, to), send_sem=send, recv_sem=recv,
            device_id={"blk": b, "head": to}, device_id_type=MESH,
        )

    def line_send(at, send, recv, d, act):
        @pl.when((z - d + 1 >= 0) & (z + 1 < n))
        def _():
            act(line_copy(at, send(0, d), recv(0, d), z - d + 1, z + 1))

        @pl.when((z + d - 1 < n) & (z >= 1))
        def _():
            act(line_copy(at, send(1, d), recv(1, d), z + d - 1, z - 1))

    def line_recv(at, send, recv, d):
        @pl.when(z - d >= 0)
        def _():
            line_copy(lambda j, _: at(j, z), send(0, d), recv(0, d), z - d, z - 1).wait_recv()

        @pl.when(z + d < n)
        def _():
            line_copy(lambda j, _: at(j, z), send(1, d), recv(1, d), z + d, z + 1).wait_recv()

    def x_line(s):
        return (
            lambda j, _: x_all.at[s, j],
            lambda way, d: xs_sem.at[s, way, d - 1],
            lambda way, d: xr_sem.at[s, way, d - 1],
        )

    w_line = (
        lambda j, at: wo.at[piece[0], lax.rem(j - at + n, n)],
        lambda way, d: ws_sem.at[way, d - 1],
        lambda way, d: wr_sem.at[way, d - 1],
    )

    def w_tree(r, back):
        step = 1 if r % 2 else low_bit(r)
        held = piece[r if back else r ^ step]
        ref = wo.at[held, pl.ds(1, n - 1)]
        return pltpu.make_async_remote_copy(
            src_ref=ref, dst_ref=ref, send_sem=ts_sem.at[r], recv_sem=tr_sem.at[r],
            device_id={"blk": flipped[step], "head": z}, device_id_type=MESH,
        )

    def route(s, r):
        if r % 2:
            return flipped[r - 1], flipped[1], flipped[r]
        first, second = low_bit(r), high_bit(r)
        odd = lax.rem(s, 2)
        blocks = [flipped[r ^ step] for step in (second, first)]
        peers = [flipped[step] for step in (second, first)]
        return (
            blocks[0] * (1 - odd) + blocks[1] * odd,
            peers[0] * (1 - odd) + peers[1] * odd,
            flipped[r],
        )

    def kv_send(s, r):
        block, peer, _ = route(s, r)
        return pltpu.make_async_remote_copy(
            src_ref=kv.at[s, block], dst_ref=kv.at[s, block],
            send_sem=ks_sem.at[s], recv_sem=kr_sem.at[s, 1 if r % 2 else r],
            device_id={"blk": peer, "head": z}, device_id_type=MESH,
        )

    def kv_recv(s, r):
        _, peer, mine = route(s, r)
        pltpu.make_async_remote_copy(
            src_ref=kv.at[s, mine], dst_ref=kv.at[s, mine],
            send_sem=ks_sem.at[s], recv_sem=kr_sem.at[s, 1 if r % 2 else r],
            device_id={"blk": peer, "head": z}, device_id_type=MESH,
        ).wait_recv()

    def gated_copy(s, o):
        to = ring[o]
        return pltpu.make_async_remote_copy(
            src_ref=gout.at[s, to], dst_ref=gin.at[s, z],
            send_sem=gs_sem.at[s], recv_sem=gr_sem.at[s],
            device_id={"blk": b, "head": to}, device_id_type=MESH,
        )

    def whole_copy(ref, send, recv, blk, head):
        return pltpu.make_async_remote_copy(
            src_ref=ref, dst_ref=ref, send_sem=send, recv_sem=recv,
            device_id={"blk": blk, "head": head}, device_id_type=MESH,
        )

    def sibling_recv(s):
        ref = kv.at[s, pl.ds(0, nb // 2)]
        whole_copy(ref, ks_sem.at[s], kr_sem.at[s, 1], flipped[1], z).wait_recv()

    def kv_sent(s):
        ref = kv.at[s, pl.ds(0, nb - 1)]
        whole_copy(ref, ks_sem.at[s], kr_sem.at[s, 1], flipped[1], z).wait_send()

    def gated_recv(s):
        ref = gin.at[s, pl.ds(0, n - 1)]
        whole_copy(ref, gs_sem.at[s], gr_sem.at[s], b, ring[1]).wait_recv()

    def gated_sent(s):
        ref = gout.at[s, pl.ds(0, n - 1)]
        whole_copy(ref, gs_sem.at[s], gr_sem.at[s], b, ring[1]).wait_send()

    rows = lax.broadcasted_iota(jnp.int32, (td, 128), 0)
    lanes = lax.broadcasted_iota(jnp.int32, (td, 128), 1)
    chains = cemb_ref.shape[0]
    chain = jnp.zeros((td, 128), jnp.int32)
    for i in range(td):
        chain = jnp.where(rows == i, chain_ref[i], chain)
    position = (b * n + z) * td + rows
    hot = jnp.zeros((td, 128), jnp.int32)
    for i in range(hot_ref.shape[0]):
        hot = jnp.where(position == hot_ref[i], 1, hot)
    picks = jnp.where(lanes == chain, 1.0, jnp.where(lanes == chains, hot.astype(jnp.float32), 0.0))
    table[...] = jnp.zeros_like(table)
    table[0:chains] = cemb_ref[...].astype(jnp.float32)
    table[chains : chains + 1] = hemb_ref[...].astype(jnp.float32).reshape(1, width)
    cond[...] = jnp.dot(
        picks.astype(jnp.bfloat16), table[...].astype(jnp.bfloat16), preferred_element_type=jnp.float32
    )

    pl.semaphore_wait(barrier, n - 1 + len(bits))

    def normalize(s):
        shifted = tok_ref[s].astype(jnp.float32) + cond[...]
        average = jnp.mean(shifted, axis=-1, keepdims=True)
        centered = shifted - average
        spread = jnp.mean(centered * centered, axis=-1, keepdims=True)
        x_all[s, z] = (centered * lax.rsqrt(spread + 1e-05)).astype(jnp.bfloat16)
        line_send(*x_line(s), 1, lambda copy: copy.start())

    early = min(2, samples)
    normalize(0)
    for copy in wo_copies:
        copy.wait()
    line_send(*w_line, 1, lambda copy: copy.start())
    for s in range(1, early):
        normalize(s)

    w_copy.wait()
    tile = 128 if w_ref.shape[1] % 128 == 0 else w_ref.shape[1]
    for c in range(0, w_ref.shape[1], tile):
        w_t[c : c + tile] = w_v[:, c : c + tile].astype(jnp.float32).T.astype(jnp.bfloat16)

    evens = [r for r in range(2, nb, 2)]
    levels = max(bin(r).count("1") for r in evens)
    attend_lag = levels + 1
    out_lag = attend_lag + 1

    per = 2
    chunks = nb // per

    def at_sample(s, act):
        @pl.when((s >= 0) & (s < samples))
        def _():
            act(s)

    def project(s):
        x = x_all[s].reshape(tb, width)
        proj = lax.dot_general(
            w_t[...], x, (((1,), (1,)), ((), ())), preferred_element_type=jnp.float32
        )
        keys, values = [], []
        for h in range(hh):
            base = h * 4 * HD
            keys.append(proj[base + HD : base + 2 * HD])
            values.append(proj[base + 2 * HD : base + 3 * HD])
        ones = jnp.ones((64 - HD, tb), jnp.float32)
        values = values + [jnp.ones((HD, tb), jnp.float32)] * (hh % 2)
        pairs = [
            jnp.concatenate([values[h], ones, values[h + 1], ones], axis=0).T
            for h in range(0, hh, 2)
        ]
        kv[s, b] = jnp.concatenate(keys + pairs, axis=0).astype(jnp.bfloat16)
        for bit in bits:
            kv_send(s, bit).start()
        for h in range(hh):
            base = h * 4 * HD
            q_all[s, h] = (proj[base : base + HD] * (LOG2E / HD**0.5)).T.astype(jnp.bfloat16)
            gate_all[s, h] = jax.nn.sigmoid(proj[base + 3 * HD : base + 4 * HD]).T

    def forward(level):
        def act(s):
            for r in evens:
                if bin(r).count("1") != level:
                    continue
                kv_recv(s, r)
                kv_send(s, r + 1).start()
                for bit in bits[1:]:
                    if r & bit:
                        continue
                    later = r | bit
                    first, second = low_bit(later), high_bit(later)
                    if bit == second:

                        @pl.when(s % 2 == 0)
                        def _(later=later):
                            kv_send(s, later).start()

                    if bit == first:

                        @pl.when(s % 2 == 1)
                        def _(later=later):
                            kv_send(s, later).start()

        return act

    def attend(s):
        sibling_recv(s)
        def chunk(h, c):
            blocks = [kv[s, a, h * HD : (h + 1) * HD, :] for a in range(c * per, (c + 1) * per)]
            return jnp.concatenate(blocks, axis=1)

        def value_pair(h, c):
            base = cols + h // 2 * tb
            blocks = [kv[s, a, base : base + tb, :] for a in range(c * per, (c + 1) * per)]
            return jnp.concatenate(blocks, axis=0)

        def score(h, c):
            here = slice(c * per * tb, (c + 1) * per * tb)
            part = jnp.dot(q_all[s, h], chunk(h, c), preferred_element_type=jnp.float32)
            part = part + bias_f[h, :, here]
            sc[h, :, here] = part
            top = part[:, :tb]
            for i in range(1, per):
                top = jnp.maximum(top, part[:, i * tb : (i + 1) * tb])
            return top

        def weigh(h, c, top):
            here = slice(c * per * tb, (c + 1) * per * tb)
            probs = jnp.exp2((sc[h, :, here] - top).astype(jnp.bfloat16))
            return jnp.dot(probs, value_pair(h, c), preferred_element_type=jnp.float32)

        parts = []
        tops = [[score(h, c) for c in range(chunks)] for h in range(hh)]
        tops = [jnp.max(functools.reduce(jnp.maximum, top), axis=-1, keepdims=True) for top in tops]
        sums = [None] * hh
        for c in range(chunks):
            for h in range(hh):
                part = weigh(h, c, tops[h])
                sums[h] = part if sums[h] is None else sums[h] + part
        for h in range(hh):
            weighted = sums[h][:, h % 2 * 64 : h % 2 * 64 + 64]
            parts.append(weighted[:, :HD] / weighted[:, HD : HD + 1] * gate_all[s, h])
        gated = jnp.concatenate(parts, axis=1)
        for j in range(n):
            gout[s, j] = gated[j * td : (j + 1) * td].astype(jnp.bfloat16)
        for o in range(1, n):
            gated_copy(s, o).start()
        gin[s, z] = gout[s, z]

    def w_forward(level):
        for r in range(2, pieces, 2):
            if bin(r).count("1") != level:
                continue
            w_tree(r, True).wait_recv()
            w_tree(r + 1, False).start()
            for bit in bits[1:]:
                if not r & bit and (r | bit) < pieces and low_bit(r | bit) == bit:
                    w_tree(r | bit, False).start()

    batch = 4 if samples % 4 == 0 else 1

    def collect(s):
        gated_recv(s)

        @pl.when(s == batch - 1)
        def _():
            for r in range(1, pieces, 2):
                w_tree(r, True).wait_recv()

        @pl.when(lax.rem(s, batch) == batch - 1)
        def _():
            here = pl.ds(s - (batch - 1), batch)
            total = [jnp.zeros((batch * td, piece_cols), jnp.float32) for _ in range(halves)]
            for j in range(n):
                share = gin[here, ring[j]].reshape(batch * td, cols)
                for half in range(halves):
                    rows = [wo[p, j] for p in range(half, pieces, halves)]
                    total[half] = total[half] + jnp.dot(
                        share, jnp.concatenate(rows, axis=0), preferred_element_type=jnp.float32
                    )
            for half in range(halves):
                part = total[half].reshape(batch, td, piece_cols).astype(out_ref.dtype)
                out_ref[here, :, half * piece_cols : (half + 1) * piece_cols] = part

    def drain(s):
        for d in range(1, n):
            line_send(*x_line(s), d, lambda copy: copy.wait_send())
        kv_sent(s)
        gated_sent(s)

    ahead = n - 2

    def step(i, carry):
        t = i - ahead
        for d in range(1, n):

            def hop(s, d=d):
                line_recv(*x_line(s), d)
                if d + 1 < n:
                    line_send(*x_line(s), d + 1, lambda copy: copy.start())

            at_sample(t + (n - 1 - d), hop)
        at_sample(t + ahead + early, normalize)
        for d in range(1, n):

            @pl.when(t == min(d, ahead + 1) - ahead - 1)
            def _(d=d):
                line_recv(*w_line, d)
                if d + 1 < n:
                    line_send(*w_line, d + 1, lambda copy: copy.start())
                else:
                    for bit in bits:
                        if bit < pieces:
                            w_tree(bit, False).start()

        for level in range(1, pieces.bit_length() - 1):

            @pl.when(t == level)
            def _(level=level):
                w_forward(level)

        at_sample(t, project)

        @pl.when(t == -1)
        def _():
            bias_copy.wait()
            for h in range(hh):
                bias_f[h] = bias_v[h].astype(jnp.float32) * LOG2E

        at_sample(t - attend_lag, attend)
        at_sample(t - out_lag, collect)
        for level in range(1, levels + 1):
            at_sample(t - level, forward(level))
        at_sample(t - out_lag, drain)
        return carry

    lax.fori_loop(0, ahead + samples + out_lag, step, 0)

    for d in range(1, n):
        line_send(*w_line, d, lambda copy: copy.wait_send())
    for r in range(1, pieces):
        w_tree(r, False).wait_send()


def body(n, nb, tokens, chain_id, hotspots, chain_embed, hot_embed, w_proj, pair_bias, w_out):
    samples, td, width = tokens.shape
    hh, tb, keys = pair_bias.shape
    cols = hh * HD
    smem = pl.BlockSpec(memory_space=pltpu.SMEM)
    vmem = pl.BlockSpec(memory_space=pltpu.VMEM)
    bf16, f32 = jnp.bfloat16, jnp.float32
    dma = pltpu.SemaphoreType.DMA
    pieces, piece_cols = 2 * hh, width // 2
    return pl.pallas_call(
        functools.partial(kernel, n, nb),
        out_shape=jax.ShapeDtypeStruct((samples, td, width), bf16),
        in_specs=[smem, smem] + [vmem] * 3 + [pl.BlockSpec(memory_space=pl.ANY)] * 3,
        out_specs=vmem,
        scratch_shapes=[
            pltpu.VMEM((samples, n, td, width), bf16),
            pltpu.VMEM((128, width), f32),
            pltpu.VMEM((td, width), f32),
            pltpu.VMEM(w_proj.shape, bf16),
            pltpu.VMEM((w_proj.shape[1], width), bf16),
            pltpu.VMEM(pair_bias.shape, bf16),
            pltpu.VMEM(pair_bias.shape, f32),
            pltpu.VMEM((hh, tb, keys), f32),
            pltpu.VMEM((samples, nb, cols + (hh + 1) // 2 * tb, tb), bf16),
            pltpu.VMEM((samples, hh, tb, HD), bf16),
            pltpu.VMEM((samples, hh, tb, HD), f32),
            pltpu.VMEM((samples, n, td, cols), bf16),
            pltpu.VMEM((samples, n, td, cols), bf16),
            pltpu.VMEM((pieces, n, HD, piece_cols), bf16),
            dma((2 + pieces,)),
            dma((samples, 2, n - 1)),
            dma((samples, 2, n - 1)),
            dma((2, n - 1)),
            dma((2, n - 1)),
            dma((pieces,)),
            dma((pieces,)),
            dma((samples,)),
            dma((samples, nb)),
            dma((samples,)),
            dma((samples,)),
        ],
        compiler_params=pltpu.CompilerParams(
            collective_id=0, has_side_effects=True, vmem_limit_bytes=56 * 1024 * 1024
        ),
    )(chain_id, hotspots, tokens, chain_embed, hot_embed, w_proj, pair_bias, w_out)


def solution(mesh):
    in_specs = (
        P(None, ("blk", "head"), None),
        P(("blk", "head")),
        P(),
        P(),
        P(),
        P(None, "head"),
        P("head", "blk", None),
        P("head", None),
    )
    out_specs = P(None, ("blk", "head"), None)
    run = functools.partial(body, mesh.shape["head"], mesh.shape["blk"])
    return jax.shard_map(run, mesh=mesh, in_specs=in_specs, out_specs=out_specs, check_vma=False)
```
